256 devices in a mesh: gx: 32 (over y, x, core), gy: 8 (over z).
Axes of the slice: x: 4, y: 4, z: 8, core: 2. Of those that a mesh axis runs over, the one named last changes fastest.
Arguments:
- grid_field: float32 [2, 64, 1024, 2048], P(None, None, 'gx', 'gy'), may hold values from -6 to 6
- coefficient: float32 [1024, 2048], P('gx', 'gy'), may hold values from 0.5 to 2
- spectral_weight: float32 [128, 128, 64, 128], P('gx', 'gy'), may hold values from -0.5 to 0.5
- local_weight: float32 [64, 64], replicated, may hold values from -0.75 to 0.75
Outputs:
- layer_out: float32 [2, 64, 1024, 2048], P(None, None, 'gx', 'gy')
The draws below stay inside these ranges and needn't reach their ends.
All inputs are finite; a program needn't handle non-finite values.
Results may differ from the reference program's by a relative error of at most 0.00005.
Values sent between devices are 32-bit elements; how exact they have to be, the bound alone decides.
A program may use at most 128 MiB of HBM per device.

```python
import math
import jax
import jax.numpy as jnp
from jax import lax

CH = 64
MX = 128
MY = 128
BATCH = 2
NX = 1024
NY = 2048


def shard_levels(own_key, shape, cuts, low, top_value):
    def one(dim, blocks):
        heights = jax.random.uniform(jax.random.fold_in(jax.random.fold_in(own_key, 6), dim), (blocks,), jnp.float32, low / len(cuts), top_value / len(cuts))
        return jnp.repeat(jnp.exp(heights), shape[dim] // blocks).reshape((-1,) + (1,) * (len(shape) - dim - 1))

    loudness = one(*cuts[0])
    for cut in cuts[1:]:
        loudness = loudness * one(*cut)
    return loudness


def gaussian(rng, extent, spread, most, shards=(), kind=jnp.bfloat16):
    result = spread * jax.random.normal(rng, extent, jnp.float32)
    if shards:
        result = result * shard_levels(rng, extent, shards, -0.22, 0.18)
    return jnp.clip(result, -most, most).astype(kind)


def setup_inputs(seed: int = 0) -> dict:
    seeds = jax.random.split(jax.random.key(seed), 5)
    grid_field = gaussian(seeds[0], (BATCH, CH, NX, NY), 1.0, 6.0, ((2, 32), (3, 8)), jnp.float32)
    coefficient = jnp.clip(jnp.exp(math.log(2.0) - 1.3862944 * jax.random.uniform(seeds[1], (NX, NY), jnp.float32) ** shard_levels(seeds[1], (NX, NY), ((0, 32), (1, 8)), -0.2, 0.2)), 0.5, 2.0)
    spectral_weight = gaussian(seeds[2], (MX, MY, CH, 2 * CH), (2 * CH) ** -0.5, 0.5, ((0, 32), (1, 8)), jnp.float32)
    local_weight = gaussian(seeds[3], (CH, CH), CH ** -0.5, 0.75, (), jnp.float32)
    return {"grid_field": grid_field, "coefficient": coefficient, "spectral_weight": spectral_weight, "local_weight": local_weight}


highest = lax.Precision.HIGHEST


def phases(position, frequency, period):
    product = (position[:, None] * frequency[None, :]) % period
    return product.astype(jnp.float32) * (2.0 * math.pi / period)


def signed_modes(index_range, count, period):
    return jnp.where(index_range < count // 2, index_range, index_range - count + period)


def reference(grid_field, coefficient, spectral_weight, local_weight):
    y_angle = phases(jnp.arange(NY, dtype=jnp.int32), jnp.arange(MY, dtype=jnp.int32), NY)
    y_cosine = jnp.cos(y_angle)
    y_sine = jnp.sin(y_angle)
    x_angle = phases(jnp.arange(NX, dtype=jnp.int32), signed_modes(jnp.arange(MX, dtype=jnp.int32), MX, NX), NX)
    x_cosine = jnp.cos(x_angle)
    x_sine = jnp.sin(x_angle)
    y_real = jnp.einsum('bcxy,yk->bcxk', grid_field, y_cosine, precision=highest)
    y_imag = -jnp.einsum('bcxy,yk->bcxk', grid_field, y_sine, precision=highest)
    z_real = jnp.einsum('xk,bcxm->bckm', x_cosine, y_real, precision=highest) + jnp.einsum('xk,bcxm->bckm', x_sine, y_imag, precision=highest)
    z_imag = jnp.einsum('xk,bcxm->bckm', x_cosine, y_imag, precision=highest) - jnp.einsum('xk,bcxm->bckm', x_sine, y_real, precision=highest)
    w_real = spectral_weight[..., :CH]
    w_imag = spectral_weight[..., CH:]
    m_real = jnp.einsum('bikm,kmio->bokm', z_real, w_real, precision=highest) - jnp.einsum('bikm,kmio->bokm', z_imag, w_imag, precision=highest)
    m_imag = jnp.einsum('bikm,kmio->bokm', z_real, w_imag, precision=highest) + jnp.einsum('bikm,kmio->bokm', z_imag, w_real, precision=highest)
    g_real = jnp.einsum('xk,bokm->boxm', x_cosine, m_real, precision=highest) - jnp.einsum('xk,bokm->boxm', x_sine, m_imag, precision=highest)
    g_imag = jnp.einsum('xk,bokm->boxm', x_sine, m_real, precision=highest) + jnp.einsum('xk,bokm->boxm', x_cosine, m_imag, precision=highest)
    y_weights = jnp.where(jnp.arange(MY) == 0, 1.0, 2.0).astype(jnp.float32) / float(NX * NY)
    spectral = jnp.einsum('boxm,ym->boxy', g_real, y_cosine * y_weights[None, :], precision=highest) - jnp.einsum('boxm,ym->boxy', g_imag, y_sine * y_weights[None, :], precision=highest)
    padded = jnp.pad(grid_field, ((0, 0), (0, 0), (1, 1), (1, 1)))
    beside_all = padded[:, :, 2:, 1:-1] + padded[:, :, :-2, 1:-1] + padded[:, :, 1:-1, 2:] + padded[:, :, 1:-1, :-2]
    stencil = coefficient * (grid_field - 0.25 * beside_all)
    pointwise = jnp.einsum('oi,bixy->boxy', local_weight, grid_field, precision=highest)
    return jax.nn.gelu(spectral + pointwise + stencil)
```

```python
import functools
import math

import jax
import jax.numpy as jnp
import ml_dtypes
import numpy as np
from jax import lax
from jax.experimental import pallas as pl
from jax.experimental.pallas import tpu as pltpu
from jax.sharding import PartitionSpec as P

MESH = pl.DeviceIdType.MESH
MX = 128
MY = 128
NX = 1024
NY = 2048
highest = lax.Precision.HIGHEST
f32 = jnp.float32
bf16 = jnp.bfloat16


def halves(table):
    table = np.asarray(table, np.float64)
    high = table.astype(np.float32).astype(ml_dtypes.bfloat16)
    low = (table - high.astype(np.float64)).astype(np.float32).astype(ml_dtypes.bfloat16)
    return np.stack([high, low], axis=-3)


def angles(position, frequency, period):
    return (np.outer(position, frequency) % period) * (2.0 * math.pi / period)


def x_frequency():
    k = np.arange(MX)
    return np.where(k < MX // 2, k, k - MX + NX)


def group_rows(axis, place):
    y, x, c, r = np.meshgrid(np.arange(4), np.arange(4), np.arange(2), np.arange(32), indexing="ij")
    row = ((y * 4 + x) * 2 + c) * 32 + r
    return (row[place] if axis == 0 else row[:, place]).reshape(-1)


def tables():
    fx = x_frequency()
    spread = (np.arange(128) % 32) * 4 + np.arange(128) // 32
    x_fwd, x_inv = [], []
    for axis in (0, 1):
        for place in range(4):
            angle = angles(group_rows(axis, place), fx, NX)
            x_fwd.append(np.concatenate([np.cos(angle).T, np.sin(angle).T], 0))
            x_inv.append(np.concatenate([np.cos(angle)[:, spread], np.sin(angle)[:, spread]], 0))
    y_fwd, y_inv_a, y_inv_b = [], [], []
    weight = np.where(np.arange(MY) == 0, 1.0, 2.0) / float(NX * NY)
    for place in range(8):
        angle = angles(place * 256 + np.arange(256), np.arange(MY), NY).T
        cosine, sine = np.cos(angle), np.sin(angle)
        y_fwd.append(
            np.stack([cosine.reshape(8, 16, 256), -sine.reshape(8, 16, 256)], 1).reshape(256, 256)
        )
        cosine, sine = cosine * weight[:, None], -sine * weight[:, None]
        y_inv_a.append(
            np.stack([cosine.reshape(8, 16, 256), sine.reshape(8, 16, 256)], 1).reshape(256, 256)
        )
        y_inv_b.append(np.concatenate([cosine, sine], 0))
    angle = angles(np.arange(NX), fx, NX)
    x_all_fwd = np.concatenate([np.cos(angle), np.sin(angle)], 1)
    x_all_inv = np.concatenate([np.cos(angle)[:, spread].T, np.sin(angle)[:, spread].T], 1)
    return [
        halves(np.stack(x_fwd)),
        halves(np.stack(x_inv)),
        halves(np.stack(y_fwd)),
        halves(np.stack(y_inv_b)),
        halves(x_all_fwd),
        halves(x_all_inv),
        halves(np.stack(y_inv_a)),
    ]


def split(value):
    high = value.astype(bf16)
    return high, (value - high.astype(f32)).astype(bf16)


def dot(a, b, dims):
    return lax.dot_general(a, b, (dims, ((), ())), preferred_element_type=f32)


NN = ((1,), (0,))
NT = ((1,), (1,))
TN = ((0,), (0,))


def dot3(a, b, dims):
    return dot(a[0], b[0], dims) + (dot(a[0], b[1], dims) + dot(a[1], b[0], dims))


def quarters(blocks):
    rows = blocks[0].shape[0]
    lane = lax.broadcasted_iota(jnp.int32, (rows, 128), 1) // 32
    out = []
    for k in range(4):
        result = blocks[k] if k == 0 else None
        for v in range(4):
            shift = (32 * (v - k)) % 128
            moved = blocks[v] if shift == 0 else pltpu.roll(blocks[v], shift, 1)
            result = moved if v == 0 else jnp.where(lane == v, moved, result)
        out.append(result)
    return out


class Place:
    def __init__(self):
        self.j = lax.axis_index("gx")
        self.d = lax.axis_index("gy")
        self.y = self.j // 8
        self.x = (self.j // 2) % 4
        self.c = self.j % 2

    def gx(self, r):
        return (
            ((self.y + r // 8) % 4) * 8 + ((self.x + (r // 2) % 4) % 4) * 2 + (self.c + r % 2) % 2
        )

    def gx_back(self, r):
        return (
            ((self.y + 4 - r // 8) % 4) * 8
            + ((self.x + 4 - (r // 2) % 4) % 4) * 2
            + (self.c + r % 2) % 2
        )

    def member(self, axis, r):
        core = (self.c + r % 2) % 2
        if axis == 0:
            place = (self.x + r // 2) % 4
            return place, core, self.y * 8 + place * 2 + core
        place = (self.y + r // 2) % 4
        return place, core, place * 8 + self.x * 2 + core

    def across(self, axis, r):
        if axis == 0:
            place = (self.y + r) % 4
            return place, place * 8 + self.x * 2 + self.c
        place = (self.x + r) % 4
        return place, self.y * 8 + place * 2 + self.c

    def gy(self, r):
        return (self.d + r + 8) % 8


CHAINS = ((1, 0, 4), (-1, 1, 4), (-1, 0, 3), (1, 1, 3))


def spectral_kernel(
    grid,
    weight,
    t_xf,
    t_xi,
    t_yf,
    t_yi,
    t_xaf,
    t_xai,
    gather,
    spec,
    xf,
    xi,
    yf,
    yi,
    xaf,
    xai,
    w,
    g0,
    part,
    ring,
    first,
    z2,
    z2r,
    z3,
    z3r,
    a_send,
    a_recv,
    m_send,
    m_recv,
    n_send,
    n_recv,
    mixed,
    b_send,
    b_recv,
    h3,
    h3r,
    h2r,
    out1,
    load,
    s_p1,
    r_p1,
    s_p2,
    r_p2,
    s_p3,
    r_p3,
    s_ring,
    r_ring,
    s_a,
    r_a,
    s_m,
    r_m,
    s_n,
    r_n,
    s_b,
    r_b,
    s_g,
    r_g,
    s_q3,
    r_q3,
    s_q2,
    r_q2,
    s_q1,
    r_q1,
    own,
):
    at = Place()
    j, d = at.j, at.d

    def remote(src, dst, send, recv, gx, gy):
        return pltpu.make_async_remote_copy(
            src_ref=src, dst_ref=dst, send_sem=send, recv_sem=recv, device_id=(gx, gy), device_id_type=MESH
        )

    loads = [
        pltpu.make_async_copy(grid.at[0], g0, load.at[0]),
        pltpu.make_async_copy(t_yf.at[d], yf, load.at[1]),
        pltpu.make_async_copy(t_xf.at[at.y], xf.at[0], load.at[2]),
        pltpu.make_async_copy(t_xf.at[4 + at.x], xf.at[1], load.at[3]),
        pltpu.make_async_copy(t_xaf, xaf, load.at[4]),
        pltpu.make_async_copy(weight, w, load.at[5]),
        pltpu.make_async_copy(t_xai, xai, load.at[6]),
        pltpu.make_async_copy(t_xi.at[at.y], xi.at[0], load.at[7]),
        pltpu.make_async_copy(t_xi.at[4 + at.x], xi.at[1], load.at[8]),
        pltpu.make_async_copy(t_yi.at[d], yi, load.at[9]),
    ]
    for copy in loads:
        copy.start()

    barrier = pltpu.get_barrier_semaphore()

    def greet(r, carry):
        pl.semaphore_signal(barrier, inc=1, device_id=(at.gx(r), d), device_id_type=MESH)
        return carry

    lax.fori_loop(1, 32, greet, 0)
    for r in range(1, 8):
        pl.semaphore_signal(barrier, inc=1, device_id=(j, at.gy(r)), device_id_type=MESH)
    pl.semaphore_wait(barrier, 31 + 7)

    def grid_piece(axis, chunk, place, core):
        if axis == 0:
            return grid.at[1, 0, pl.ds(2 * chunk, 2), place, core]
        return grid.at[1, 1, place, pl.ds(2 * chunk, 2), core]

    def p1(axis, chunk, r):
        place, core, gx = at.member(axis, r)
        mine = (at.x if axis == 0 else at.y) * 2 + at.c
        return remote(
            grid_piece(axis, chunk, place, core),
            first.at[axis, pl.ds(2 * chunk, 2), mine],
            s_p1.at[axis, chunk, r],
            r_p1.at[axis, chunk, r],
            gx,
            d,
        )

    def p1_own(axis, chunk):
        place = at.x if axis == 0 else at.y
        return pltpu.make_async_copy(
            grid_piece(axis, chunk, place, at.c),
            first.at[axis, pl.ds(2 * chunk, 2), place * 2 + at.c],
            own.at[axis, chunk],
        )

    for chunk in range(2):
        for r in (2, 6, 3, 7, 4, 5, 1):
            for axis in range(2):
                p1(axis, chunk, r).start()
        for axis in range(2):
            p1_own(axis, chunk).start()

    loads[0].wait()
    loads[1].wait()

    def columns(half, carry):
        for k in range(4):
            t = half * 8 + 2 * k
            rows = []
            for tile in range(2):
                own_of = t + tile
                for core in range(2):
                    for low in range(2):
                        rows.append(g0[low, own_of // 4, own_of % 4, core])
            block = split(jnp.concatenate(rows, axis=0))
            result = dot3((yf[0], yf[1]), block, NT)
            for e in range(8):
                part[e, half, :, 256 * k : 256 * k + 256] = result[32 * e : 32 * e + 32]
        return carry

    def hop(chain, s):
        direction, half, hops = CHAINS[chain]
        to = at.gy(direction * (hops - s))
        return remote(
            part.at[to, half],
            ring.at[chain, s],
            s_ring.at[chain, s],
            r_ring.at[chain, s],
            j,
            at.gy(direction),
        )

    def collect(s):
        for chain in range(4):
            direction, half, hops = CHAINS[chain]
            if s < hops:
                hop(chain, s).wait_recv()
                to = at.gy(direction * (hops - 1 - s))
                part[to, half] = part[to, half] + ring[chain, s]
                if s + 1 < hops:
                    hop(chain, s + 1).start()

    columns(0, 0)
    for chain in (0, 2):
        hop(chain, 0).start()
    columns(1, 0)
    for chain in (1, 3):
        hop(chain, 0).start()

    loads[2].wait()
    loads[3].wait()

    def modes_of(axis, channel):
        block = split(first[axis, channel].reshape(256, 256))
        rows = split(dot3((xf[axis, 0], xf[axis, 1]), block, NN))
        both = dot3((yf[0], yf[1]), rows, NT)
        for e in range(8):
            cos_y = both[32 * e : 32 * e + 16]
            sin_y = both[32 * e + 16 : 32 * e + 32]
            z2[axis, channel, e, 0] = cos_y[:, :128] + sin_y[:, 128:]
            z2[axis, channel, e, 1] = sin_y[:, :128] - cos_y[:, 128:]

    def p2(axis, r):
        place, gx = at.across(axis, r)
        return remote(
            z2.at[axis, place], z2r.at[axis, r], s_p2.at[axis, r], r_p2.at[axis, r], gx, d
        )

    def forward_chunk(axis, chunk):
        for r in range(1, 8):
            p1(axis, chunk, r).wait_recv()
        p1_own(axis, chunk).wait()

        def one(k, carry):
            modes_of(axis, 2 * chunk + k)
            return carry

        lax.fori_loop(0, 2, one, 0)

    collect(0)
    for axis in range(2):
        forward_chunk(axis, 0)
    collect(1)
    for axis in range(2):
        forward_chunk(axis, 1)
        for r in (1, 3, 2):
            p2(axis, r).start()
    collect(2)

    for axis in range(2):
        for r in range(1, 4):
            p2(axis, r).wait_recv()
        place = at.y if axis == 0 else at.x
        for e in range(8):
            z3[e, axis] = (z2[axis, place, e] + z2r[axis, 1, e]) + (z2r[axis, 2, e] + z2r[axis, 3, e])

    def p3(r):
        to = at.gy(r)
        return remote(z3.at[to], z3r.at[r], s_p3.at[r], r_p3.at[r], j, to)

    for r in (4, 3, 5, 2, 6, 1, 7):
        p3(r).start()
    collect(3)

    lane = lax.broadcasted_iota(jnp.int32, (16, 128), 1)
    for t in range(16):
        here = pl.ds(128 * (t % 8), 128)
        real = part[d, t // 8, 0:16, here]
        imag = part[d, t // 8, 16:32, here]
        a_send[2 * t] = jnp.where(lane < 64, real, pltpu.roll(imag, 64, 1))
        a_send[2 * t + 1] = jnp.where(lane < 64, pltpu.roll(real, 64, 1), imag)

    def spread_copy(send, recv, s_sem, r_sem, r):
        gx = at.gx(r)
        return remote(send.at[gx], recv.at[j], s_sem.at[r], r_sem.at[r], gx, d)

    def spread_start(*refs):
        def start(r, carry):
            spread_copy(*refs, r).start()
            return carry

        lax.fori_loop(1, 32, start, 0)
        send, recv = refs[:2]
        recv[j] = send[j]

    def spread_wait(*refs):
        def wait(r, carry):
            spread_copy(*refs, r).wait_recv()
            return carry

        lax.fori_loop(1, 32, wait, 0)

    a_refs = (a_send, a_recv, s_a, r_a)
    spread_start(*a_refs)

    for r in range(1, 8):
        p3(r).wait_recv()
    stack = []
    for axis in range(2):
        total = z3[d, axis]
        for r in range(1, 8):
            total = total + z3r[r, axis]
        stack.append(total.reshape(32, 128))

    loads[4].wait()
    spread_wait(*a_refs)
    turned = [quarters([a_recv[4 * u + v] for v in range(4)]) for u in range(8)]
    rows = jnp.concatenate(
        [jnp.concatenate([turned[u][k] for u in range(8)], axis=1) for k in range(4)], axis=0
    )
    both = dot3(split(rows), (xaf[0], xaf[1]), NN)
    for half in range(2):
        real = both[16 * half : 16 * half + 16]
        imag = both[32 + 16 * half : 32 + 16 * half + 16]
        stack.append(real[:, :128] + imag[:, 128:])
        stack.append(imag[:, :128] - real[:, 128:])
    modes = jnp.concatenate(stack, axis=0).T
    for owner in range(32):
        m_send[owner] = modes[4 * owner : 4 * owner + 4]

    m_refs = (m_send, m_recv, s_m, r_m)
    spread_start(*m_refs)
    loads[5].wait()
    spread_wait(*m_refs)

    sign = jnp.where(lax.broadcasted_iota(jnp.int32, (8, 128), 1) < 64, -1.0, 1.0)

    def mix(kx, carry):
        held = m_recv[:, kx, :]
        for sample in range(2):
            rows = []
            for ky in range(16):
                from_real = jnp.zeros((32, 128), f32)
                from_imag = jnp.zeros((32, 128), f32)
                for half in range(2):
                    first_lane = (64 if sample == 0 else 0) + 32 * half + ky
                    block = w[kx, ky, 32 * half : 32 * half + 32, :]
                    from_real += held[:, first_lane : first_lane + 1] * block
                    from_imag += held[:, first_lane + 16 : first_lane + 17] * block
                from_real = (from_real[0:8] + from_real[8:16]) + (from_real[16:24] + from_real[24:32])
                from_imag = (from_imag[0:8] + from_imag[8:16]) + (from_imag[16:24] + from_imag[24:32])
                both = from_real + sign * pltpu.roll(from_imag, 64, 1)
                rows.append(jnp.sum(both, axis=0, keepdims=True))
            mixed[pl.ds(64 * sample + 16 * kx, 16), :] = jnp.concatenate(rows, axis=0)
        return carry

    lax.fori_loop(0, 4, mix, 0)
    turned_modes = mixed[...].T
    for k in range(4):
        n_send[:, k, :] = turned_modes[32 * k : 32 * k + 32]

    n_refs = (n_send, n_recv, s_n, r_n)
    spread_start(*n_refs)
    loads[6].wait()
    spread_wait(*n_refs)

    back = jnp.concatenate([n_recv[:, k, :] for k in range(4)], axis=0).T
    by_sample = []
    for sample in range(2):
        by_sample.append(
            quarters([back[64 * sample + 16 * v : 64 * sample + 16 * v + 16] for v in range(4)])
        )

    for axis in range(2):
        for k in range(2):
            h3[axis, k] = by_sample[1][2 * k + axis]

    def q3(r):
        return remote(h3, h3r.at[d], s_q3.at[r], r_q3.at[r], j, at.gy(r))

    for r in (4, 3, 5, 2, 6, 1, 7):
        q3(r).start()
    h3r[d] = h3[...]

    full = dot3(split(jnp.concatenate(by_sample[0], axis=0)), (xai[0], xai[1]), NN)
    real, imag = full[0:32], full[32:64]
    g_real = real[:, :1024] - imag[:, 1024:]
    g_imag = real[:, 1024:] + imag[:, :1024]
    for u in range(8):
        here = slice(128 * u, 128 * u + 128)
        pieces = quarters(
            [g_real[0:16, here], g_real[16:32, here], g_imag[0:16, here], g_imag[16:32, here]]
        )
        for v in range(4):
            b_send[4 * u + v] = pieces[v]
    b_refs = (b_send, b_recv, s_b, r_b)
    spread_start(*b_refs)

    for r in range(1, 8):
        q3(r).wait_recv()

    def q2(axis, r):
        place, gx = at.across(axis, r)
        mine = at.y if axis == 0 else at.x
        return remote(
            h3r.at[:, axis], h2r.at[axis, mine], s_q2.at[axis, r], r_q2.at[axis, r], gx, d
        )

    for r in (1, 3, 2):
        for axis in range(2):
            q2(axis, r).start()
    h2r[0, at.y] = h3r[:, 0]
    h2r[1, at.x] = h3r[:, 1]

    spread_wait(*b_refs)
    for t in range(16):
        even, odd = b_recv[2 * t], b_recv[2 * t + 1]
        here = pl.ds(128 * (t % 8), 128)
        part[d, t // 8, 0:16, here] = jnp.where(lane < 64, even, pltpu.roll(odd, 64, 1))
        part[d, t // 8, 16:32, here] = jnp.where(lane < 64, pltpu.roll(even, 64, 1), odd)

    def lap(chain, s):
        direction, half, hops = CHAINS[chain]
        block = at.gy(-direction * s)
        src = part.at[block, half] if s == 0 else gather.at[block, half]
        return remote(
            src,
            gather.at[block, half],
            s_g.at[chain, s],
            r_g.at[chain, s],
            j,
            at.gy(direction),
        )

    def pass_on(s):
        for chain in range(4):
            hops = CHAINS[chain][2]
            if s < hops:
                lap(chain, s).wait_recv()
                if s + 1 < hops:
                    lap(chain, s + 1).start()

    for chain in range(4):
        lap(chain, 0).start()
    keep = pltpu.make_async_copy(part.at[d], gather.at[d], own.at[0, 0])
    keep.start()

    for k in range(7, 10):
        loads[k].wait()

    def rows_of(axis, channel):
        real = jnp.concatenate([h2r[axis, channel, e, 0] for e in range(8)], axis=0)
        imag = jnp.concatenate([h2r[axis, channel, e, 1] for e in range(8)], axis=0)
        both = dot3((xi[axis, 0], xi[axis, 1]), split(jnp.concatenate([real, imag], axis=0)), NT)
        g_real = both[:256, :128] - both[256:, 128:]
        g_imag = both[256:, :128] + both[:256, 128:]
        wide = split(jnp.concatenate([g_real, g_imag], axis=1))
        out1[axis, channel] = dot3(wide, (yi[0], yi[1]), NN).reshape(8, 32, 256)

    def spec_piece(axis, chunk):
        if axis == 0:
            return spec.at[0, pl.ds(2 * chunk, 2), at.x, at.c]
        return spec.at[1, at.y, pl.ds(2 * chunk, 2), at.c]

    def q1(axis, chunk, r):
        place, core, gx = at.member(axis, r)
        return remote(
            out1.at[axis, pl.ds(2 * chunk, 2), place * 2 + core],
            spec_piece(axis, chunk),
            s_q1.at[axis, chunk, r],
            r_q1.at[axis, chunk, r],
            gx,
            d,
        )

    def q1_own(axis, chunk):
        place = at.x if axis == 0 else at.y
        return pltpu.make_async_copy(
            out1.at[axis, pl.ds(2 * chunk, 2), place * 2 + at.c],
            spec_piece(axis, chunk),
            own.at[axis, 2 + chunk],
        )

    def inverse_chunk(axis, chunk):
        def one(k, carry):
            rows_of(axis, 2 * chunk + k)
            return carry

        lax.fori_loop(0, 2, one, 0)
        for r in (2, 6, 3, 7, 4, 5, 1):
            q1(axis, chunk, r).start()
        q1_own(axis, chunk).start()

    for axis in range(2):
        for r in range(1, 4):
            q2(axis, r).wait_recv()
    for axis in range(2):
        inverse_chunk(axis, 0)
    pass_on(0)
    for axis in range(2):
        inverse_chunk(axis, 1)
    pass_on(1)
    pass_on(2)
    pass_on(3)
    for chunk in range(2):
        for axis in range(2):
            for r in range(1, 8):
                q1(axis, chunk, r).wait_recv()
            q1_own(axis, chunk).wait()
    keep.wait()

    for chunk in range(2):
        for axis in range(2):
            for r in range(1, 8):
                p1(axis, chunk, r).wait_send()
                q1(axis, chunk, r).wait_send()
    for axis in range(2):
        for r in range(1, 4):
            p2(axis, r).wait_send()
            q2(axis, r).wait_send()
    for r in range(1, 8):
        p3(r).wait_send()
        q3(r).wait_send()
    for chain in range(4):
        for s in range(CHAINS[chain][2]):
            hop(chain, s).wait_send()
            lap(chain, s).wait_send()

    def sent(r, carry):
        for refs in (a_refs, m_refs, n_refs, b_refs):
            spread_copy(*refs, r).wait_send()
        return carry

    lax.fori_loop(1, 32, sent, 0)


def spectral_call(grid_field, spectral_weight, consts):
    dma = pltpu.SemaphoreType.DMA
    vmem = pltpu.VMEM
    scratch = [
        vmem((2, 2, 256, 256), bf16),
        vmem((2, 2, 512, 128), bf16),
        vmem((2, 256, 256), bf16),
        vmem((2, 256, 256), bf16),
        vmem((2, 1024, 256), bf16),
        vmem((2, 128, 2048), bf16),
        vmem((4, 16, 64, 128), f32),
        vmem((2, 4, 4, 2, 32, 256), f32),
        vmem((8, 2, 32, 1024), f32),
        vmem((4, 4, 32, 1024), f32),
        vmem((2, 4, 8, 32, 256), f32),
        vmem((2, 4, 8, 2, 16, 128), f32),
        vmem((2, 4, 8, 2, 16, 128), f32),
        vmem((8, 2, 2, 16, 128), f32),
        vmem((8, 2, 2, 16, 128), f32),
        vmem((32, 16, 128), f32),
        vmem((32, 16, 128), f32),
        vmem((32, 4, 128), f32),
        vmem((32, 4, 128), f32),
        vmem((32, 4, 128), f32),
        vmem((32, 4, 128), f32),
        vmem((128, 128), f32),
        vmem((32, 16, 128), f32),
        vmem((32, 16, 128), f32),
        vmem((2, 2, 16, 128), f32),
        vmem((8, 2, 2, 16, 128), f32),
        vmem((2, 4, 8, 2, 16, 128), f32),
        vmem((2, 4, 8, 32, 256), f32),
        dma((10,)),
        dma((2, 2, 8)),
        dma((2, 2, 8)),
        dma((2, 4)),
        dma((2, 4)),
        dma((8,)),
        dma((8,)),
        dma((4, 4)),
        dma((4, 4)),
        *[dma((32,)) for _ in range(8)],
        dma((4, 4)),
        dma((4, 4)),
        dma((8,)),
        dma((8,)),
        dma((2, 4)),
        dma((2, 4)),
        dma((2, 2, 8)),
        dma((2, 2, 8)),
        dma((2, 4)),
    ]
    hbm = pl.BlockSpec(memory_space=pl.ANY)
    return pl.pallas_call(
        spectral_kernel,
        out_shape=(
            jax.ShapeDtypeStruct((8, 2, 32, 1024), f32),
            jax.ShapeDtypeStruct((2, 4, 4, 2, 32, 256), f32),
        ),
        in_specs=[hbm] * 8,
        out_specs=(hbm, hbm),
        scratch_shapes=scratch,
        compiler_params=pltpu.CompilerParams(
            collective_id=0, has_side_effects=True, vmem_limit_bytes=48 << 20
        ),
        name="spectral",
    )(grid_field, spectral_weight, *consts)


def padded_2(block, sides, width):
    for axis, dim in sides:
        count = lax.axis_size(axis)
        forward = [(i, i + 1) for i in range(count - 1)]
        backward = [(target, source) for source, target in forward]
        low = lax.ppermute(
            lax.slice_in_dim(block, block.shape[dim] - width, None, axis=dim), axis, forward
        )
        high = lax.ppermute(lax.slice_in_dim(block, 0, width, axis=dim), axis, backward)
        block = jnp.concatenate([low, block, high], axis=dim)
    return block


def shards(consts, grid_field, coefficient, spectral_weight, local_weight):
    consts = [jnp.asarray(c) for c in consts]
    view = grid_field.reshape(2, 2, 4, 4, 2, 32, 256)
    gather, spec = spectral_call(view, spectral_weight, consts[:6])
    y_inv = consts[6][lax.axis_index("gy")].astype(f32)
    y_inv = y_inv[0] + y_inv[1]
    low = jnp.einsum("dhkl,dky->hly", gather, y_inv.reshape(8, 32, 256), precision=highest)
    low = low.reshape(2, 8, 2, 2, 32, 256)
    low = jnp.transpose(low, (3, 0, 1, 2, 4, 5)).reshape(64, 32, 256)
    spectral = jnp.stack([low, spec.reshape(64, 32, 256)])
    padded = padded_2(grid_field, (("gx", 2), ("gy", 3)), 1)
    beside_all = (
        padded[:, :, 2:, 1:-1]
        + padded[:, :, :-2, 1:-1]
        + padded[:, :, 1:-1, 2:]
        + padded[:, :, 1:-1, :-2]
    )
    stencil = coefficient * (grid_field - 0.25 * beside_all)
    pointwise = jnp.einsum("oi,bixy->boxy", local_weight, grid_field, precision=highest)
    return jax.nn.gelu(spectral + pointwise + stencil)


def solution(mesh):
    consts = tables()
    placed = (P(None, None, "gx", "gy"), P("gx", "gy"), P("gx", "gy", None, None), P())
    return jax.shard_map(
        functools.partial(shards, consts),
        mesh=mesh,
        in_specs=placed,
        out_specs=P(None, None, "gx", "gy"),
        check_vma=False,
    )
```

```python
import functools
import math

import jax
import jax.numpy as jnp
import ml_dtypes
import numpy as np
from jax import lax
from jax.experimental import pallas as pl
from jax.experimental.pallas import tpu as pltpu
from jax.sharding import PartitionSpec as P

MESH = pl.DeviceIdType.MESH
MX = 128
MY = 128
NX = 1024
NY = 2048
f32 = jnp.float32
bf16 = jnp.bfloat16


def halves(table):
    table = np.asarray(table, np.float64)
    high = table.astype(np.float32).astype(ml_dtypes.bfloat16)
    low = (table - high.astype(np.float64)).astype(np.float32).astype(ml_dtypes.bfloat16)
    return np.stack([high, low], axis=-3)


def angles(position, frequency, period):
    return (np.outer(position, frequency) % period) * (2.0 * math.pi / period)


def x_frequency():
    k = np.arange(MX)
    return np.where(k < MX // 2, k, k - MX + NX)


def group_rows(axis, place):
    y, x, c, r = np.meshgrid(np.arange(4), np.arange(4), np.arange(2), np.arange(32), indexing="ij")
    row = ((y * 4 + x) * 2 + c) * 32 + r
    return (row[place] if axis == 0 else row[:, place]).reshape(-1)


def tables():
    fx = x_frequency()
    spread = (np.arange(128) % 32) * 4 + np.arange(128) // 32
    x_fwd, x_inv = [], []
    for axis in (0, 1):
        for place in range(4):
            angle = angles(group_rows(axis, place), fx, NX)
            x_fwd.append(np.concatenate([np.cos(angle).T, np.sin(angle).T], 0))
            x_inv.append(np.concatenate([np.cos(angle)[:, spread], np.sin(angle)[:, spread]], 0))
    y_fwd, y_inv_a, y_inv_b = [], [], []
    weight = np.where(np.arange(MY) == 0, 1.0, 2.0) / float(NX * NY)
    for place in range(8):
        angle = angles(place * 256 + np.arange(256), np.arange(MY), NY).T
        cosine, sine = np.cos(angle), np.sin(angle)
        y_fwd.append(
            np.stack([cosine.reshape(8, 16, 256), -sine.reshape(8, 16, 256)], 1).reshape(256, 256)
        )
        cosine, sine = cosine * weight[:, None], -sine * weight[:, None]
        y_inv_a.append(
            np.stack([cosine.reshape(8, 16, 256), sine.reshape(8, 16, 256)], 1).reshape(256, 256)
        )
        y_inv_b.append(np.concatenate([cosine, sine], 0))
    angle = angles(np.arange(NX), fx, NX)
    x_all_fwd = np.concatenate([np.cos(angle), np.sin(angle)], 1)
    x_all_inv = np.concatenate([np.cos(angle)[:, spread].T, np.sin(angle)[:, spread].T], 1)
    return [
        halves(np.stack(x_fwd)),
        halves(np.stack(x_inv)),
        halves(np.stack(y_fwd)),
        halves(np.stack(y_inv_b)),
        halves(x_all_fwd),
        halves(x_all_inv),
        halves(np.stack(y_inv_a)).reshape(8, 2, 8, 32, 256),
    ]


def split(value):
    high = value.astype(bf16)
    return high, (value - high.astype(f32)).astype(bf16)


def dot(a, b, dims):
    return lax.dot_general(a, b, (dims, ((), ())), preferred_element_type=f32)


NN = ((1,), (0,))
NT = ((1,), (1,))
TN = ((0,), (0,))


def dot3(a, b, dims):
    return dot(a[0], b[0], dims) + (dot(a[0], b[1], dims) + dot(a[1], b[0], dims))


def quarters(blocks):
    rows = blocks[0].shape[0]
    lane = lax.broadcasted_iota(jnp.int32, (rows, 128), 1) // 32
    out = []
    for k in range(4):
        result = blocks[k] if k == 0 else None
        for v in range(4):
            shift = (32 * (v - k)) % 128
            moved = blocks[v] if shift == 0 else pltpu.roll(blocks[v], shift, 1)
            result = moved if v == 0 else jnp.where(lane == v, moved, result)
        out.append(result)
    return out


class Place:
    def __init__(self):
        self.j = lax.axis_index("gx")
        self.d = lax.axis_index("gy")
        self.y = self.j // 8
        self.x = (self.j // 2) % 4
        self.c = self.j % 2

    def gx(self, r):
        return (
            ((self.y + r // 8) % 4) * 8 + ((self.x + (r // 2) % 4) % 4) * 2 + (self.c + r % 2) % 2
        )

    def gx_back(self, r):
        return (
            ((self.y + 4 - r // 8) % 4) * 8
            + ((self.x + 4 - (r // 2) % 4) % 4) * 2
            + (self.c + r % 2) % 2
        )

    def member(self, axis, r):
        core = (self.c + r % 2) % 2
        if axis == 0:
            place = (self.x + r // 2) % 4
            return place, core, self.y * 8 + place * 2 + core
        place = (self.y + r // 2) % 4
        return place, core, place * 8 + self.x * 2 + core

    def across(self, axis, r):
        if axis == 0:
            place = (self.y + r) % 4
            return place, place * 8 + self.x * 2 + self.c
        place = (self.x + r) % 4
        return place, self.y * 8 + place * 2 + self.c

    def gy(self, r):
        return (self.d + r + 8) % 8


CHAINS = ((1, 0, 4), (-1, 1, 4), (-1, 0, 3), (1, 1, 3))


def spectral_kernel(
    grid,
    flat,
    weight,
    local_weight,
    coefficient,
    t_xf,
    t_xi,
    t_yf,
    t_yi,
    t_xaf,
    t_xai,
    t_yia,
    result,
    xf,
    xi,
    yf,
    yi,
    yia,
    xaf,
    xai,
    w,
    w_high,
    w_low,
    wide,
    lw,
    coef,
    g,
    u,
    row_send,
    row_recv,
    col_send,
    col_recv,
    part,
    ring,
    first,
    z2,
    z2r,
    z3,
    z3r,
    a_send,
    a_recv,
    m_send,
    m_recv,
    n_send,
    n_recv,
    mixed,
    b_send,
    b_recv,
    h3,
    h3r,
    h2r,
    out1,
    gather,
    spec,
    load,
    s_p1,
    r_p1,
    s_p2,
    r_p2,
    s_p3,
    r_p3,
    s_ring,
    r_ring,
    s_a,
    r_a,
    s_m,
    r_m,
    s_n,
    r_n,
    s_b,
    r_b,
    s_g,
    r_g,
    s_q3,
    r_q3,
    s_q2,
    r_q2,
    s_q1,
    r_q1,
    s_row,
    r_row,
    s_col,
    r_col,
    own,
    done,
):
    at = Place()
    j, d = at.j, at.d

    def remote(src, dst, send, recv, gx, gy):
        return pltpu.make_async_remote_copy(
            src_ref=src, dst_ref=dst, send_sem=send, recv_sem=recv, device_id=(gx, gy), device_id_type=MESH
        )

    loads = [
        pltpu.make_async_copy(flat.at[pl.ds(0, 64)], g.at[pl.ds(0, 64)], load.at[0]),
        pltpu.make_async_copy(t_yf.at[d], yf, load.at[1]),
        pltpu.make_async_copy(t_xf.at[at.y], xf.at[0], load.at[2]),
        pltpu.make_async_copy(t_xf.at[4 + at.x], xf.at[1], load.at[3]),
        pltpu.make_async_copy(t_xaf, xaf, load.at[4]),
        pltpu.make_async_copy(weight, w, load.at[5]),
        pltpu.make_async_copy(t_xai, xai, load.at[6]),
        pltpu.make_async_copy(t_xi.at[at.y], xi.at[0], load.at[7]),
        pltpu.make_async_copy(t_xi.at[4 + at.x], xi.at[1], load.at[8]),
        pltpu.make_async_copy(t_yi.at[d], yi, load.at[9]),
        pltpu.make_async_copy(local_weight, lw, load.at[10]),
        pltpu.make_async_copy(flat.at[pl.ds(64, 64)], g.at[pl.ds(64, 64)], load.at[11]),
        pltpu.make_async_copy(coefficient, coef, load.at[12]),
        pltpu.make_async_copy(t_yia.at[d], yia, load.at[13]),
    ]
    for copy in loads:
        copy.start()

    pending = []

    def finish():
        for wait in pending:
            wait()

    def send(copy):
        copy.start()
        pending.append(copy.wait_send)

    barrier = pltpu.get_barrier_semaphore()

    def greet(r, carry):
        pl.semaphore_signal(barrier, inc=1, device_id=(at.gx(r), d), device_id_type=MESH)
        return carry

    lax.fori_loop(1, 32, greet, 0)
    for r in range(1, 8):
        pl.semaphore_signal(barrier, inc=1, device_id=(j, at.gy(r)), device_id_type=MESH)
    pl.semaphore_wait(barrier, 31 + 7)

    def grid_piece(axis, chunk, place, core):
        if axis == 0:
            return grid.at[1, 0, pl.ds(2 * chunk, 2), place, core]
        return grid.at[1, 1, place, pl.ds(2 * chunk, 2), core]

    def p1(axis, chunk, r):
        place, core, gx = at.member(axis, r)
        mine = (at.x if axis == 0 else at.y) * 2 + at.c
        return remote(
            grid_piece(axis, chunk, place, core),
            first.at[axis, pl.ds(2 * chunk, 2), mine],
            s_p1.at[axis, chunk, r],
            r_p1.at[axis, chunk, r],
            gx,
            d,
        )

    def p1_own(axis, chunk):
        place = at.x if axis == 0 else at.y
        return pltpu.make_async_copy(
            grid_piece(axis, chunk, place, at.c),
            first.at[axis, pl.ds(2 * chunk, 2), place * 2 + at.c],
            own.at[axis, chunk],
        )

    for chunk in range(2):
        for r in (2, 6, 3, 7, 4, 5, 1):
            for axis in range(2):
                send(p1(axis, chunk, r))
        for axis in range(2):
            p1_own(axis, chunk).start()

    loads[0].wait()
    loads[1].wait()

    def columns(half, carry):
        for k in range(4):
            t = half * 8 + 2 * k
            rows = []
            for tile in range(2):
                own_of = t + tile
                for core in range(2):
                    for low in range(2):
                        rows.append(g[2 * own_of + core + 32 * low])
            block = split(jnp.concatenate(rows, axis=0))
            result = dot3((yf[0], yf[1]), block, NT)
            for e in range(8):
                part[e, half, :, 256 * k : 256 * k + 256] = result[32 * e : 32 * e + 32]
        return carry

    def hop(chain, s):
        direction, half, hops = CHAINS[chain]
        to = at.gy(direction * (hops - s))
        return remote(
            part.at[to, half],
            ring.at[chain, s],
            s_ring.at[chain, s],
            r_ring.at[chain, s],
            j,
            at.gy(direction),
        )

    def collect(s):
        for chain in range(4):
            direction, half, hops = CHAINS[chain]
            if s < hops:
                hop(chain, s).wait_recv()
                to = at.gy(direction * (hops - 1 - s))
                part[to, half] = part[to, half] + ring[chain, s]
                if s + 1 < hops:
                    send(hop(chain, s + 1))

    columns(0, 0)
    for chain in (0, 2):
        send(hop(chain, 0))
    columns(1, 0)
    for chain in (1, 3):
        send(hop(chain, 0))

    def halo_row(k):
        to = (j + 31 + 2 * k) % 32
        return remote(row_send.at[k], row_recv.at[k], s_row.at[k], r_row.at[k], to, d)

    def halo_col(k):
        return remote(
            col_send.at[k], col_recv.at[k], s_col.at[k], r_col.at[k], j, at.gy(2 * k - 1)
        )

    loads[11].wait()
    for k in range(2):
        row_send[k] = g[:, 31 * k, :]
        send(halo_row(k))
    edge = lax.broadcasted_iota(jnp.int32, (16, 256), 0) * 255
    pick = jnp.where(lax.broadcasted_iota(jnp.int32, (16, 256), 1) == edge, 1.0, 0.0).astype(bf16)

    def edges(k, carry):
        high, low = split(g[pl.ds(8 * k, 8)].reshape(256, 256))
        found = dot(pick, high, NT) + dot(pick, low, NT)
        col_send[0, k] = found[0:1]
        col_send[1, k] = found[1:2]
        return carry

    lax.fori_loop(0, 16, edges, 0)
    for k in range(2):
        send(halo_col(k))

    loads[10].wait()
    spread_row = lax.broadcasted_iota(jnp.int32, (512, 64), 0) // 8
    repeat = jnp.where(
        spread_row == lax.broadcasted_iota(jnp.int32, (512, 64), 1), 1.0, 0.0
    ).astype(bf16)
    for part_of, piece in enumerate(split(lw[...])):
        tall = dot(repeat, piece, NN).astype(bf16)
        for k in range(4):
            block = dot(tall[128 * k : 128 * k + 128], repeat, NT)
            same = (lax.broadcasted_iota(jnp.int32, (128, 512), 0) % 8) == (
                lax.broadcasted_iota(jnp.int32, (128, 512), 1) % 8
            )
            wide[part_of, 128 * k : 128 * k + 128, :] = jnp.where(same, block, 0.0).astype(bf16)

    def pointwise(k, carry):
        sample, rest = k // 4, k % 4
        first_row = pl.multiple_of(8 * rest, 8)
        block = split(g[pl.ds(64 * sample, 64), pl.ds(first_row, 8), :].reshape(512, 256))
        for half in range(2):
            mine = (
                wide[0, 256 * half : 256 * half + 256],
                wide[1, 256 * half : 256 * half + 256],
            )
            u[pl.ds(64 * sample + 32 * half, 32), pl.ds(first_row, 8), :] = dot3(
                mine, block, NN
            ).reshape(32, 8, 256)
        return carry

    row_of = lax.broadcasted_iota(jnp.int32, (8, 32, 256), 1)
    lane_of = lax.broadcasted_iota(jnp.int32, (256, 256), 1)

    def stencil(k, carry):
        here = pl.ds(8 * k, 8)
        block = g[here]
        square = block.reshape(256, 256)
        has_up = jnp.where(j > 0, 1.0, 0.0)
        has_down = jnp.where(j < 31, 1.0, 0.0)
        has_left = jnp.where(d > 0, 1.0, 0.0)
        has_right = jnp.where(d < 7, 1.0, 0.0)
        up = pltpu.roll(square, 1, 0).reshape(8, 32, 256)
        down = pltpu.roll(square, 255, 0).reshape(8, 32, 256)
        above = (row_recv[1, here] * has_up)[:, None, :]
        below = (row_recv[0, here] * has_down)[:, None, :]
        up = jnp.where(row_of == 0, jnp.broadcast_to(above, up.shape), up)
        down = jnp.where(row_of == 31, jnp.broadcast_to(below, up.shape), down)
        sides = jnp.concatenate(
            [
                col_recv[1, k] * has_left,
                col_recv[0, k] * has_right,
                jnp.zeros((6, 256), f32),
            ],
            axis=0,
        ).T
        left = jnp.where(lane_of == 0, sides[:, 0:1], pltpu.roll(square, 1, 1))
        right = jnp.where(lane_of == 255, sides[:, 1:2], pltpu.roll(square, 255, 1))
        beside = (up + down) + (left + right).reshape(8, 32, 256)
        u[here] = u[here] + coef[...][None] * (block - 0.25 * beside)
        return carry

    loads[2].wait()
    loads[3].wait()

    def modes_of(axis, channel):
        block = split(first[axis, channel].reshape(256, 256))
        rows = split(dot3((xf[axis, 0], xf[axis, 1]), block, NN))
        both = dot3((yf[0], yf[1]), rows, NT)
        for e in range(8):
            cos_y = both[32 * e : 32 * e + 16]
            sin_y = both[32 * e + 16 : 32 * e + 32]
            z2[axis, channel, e, 0] = cos_y[:, :128] + sin_y[:, 128:]
            z2[axis, channel, e, 1] = sin_y[:, :128] - cos_y[:, 128:]

    def p2(axis, r):
        place, gx = at.across(axis, r)
        return remote(
            z2.at[axis, place], z2r.at[axis, r], s_p2.at[axis, r], r_p2.at[axis, r], gx, d
        )

    def forward_chunk(axis, chunk):
        for r in range(1, 8):
            p1(axis, chunk, r).wait_recv()
        p1_own(axis, chunk).wait()

        def one(k, carry):
            modes_of(axis, 2 * chunk + k)
            return carry

        lax.fori_loop(0, 2, one, 0)

    lax.fori_loop(0, 4, pointwise, 0)
    collect(0)
    lax.fori_loop(4, 8, pointwise, 0)
    for axis in range(2):
        forward_chunk(axis, 0)
    collect(1)
    for axis in range(2):
        forward_chunk(axis, 1)
        for r in (1, 3, 2):
            send(p2(axis, r))
    collect(2)

    for axis in range(2):
        for r in range(1, 4):
            p2(axis, r).wait_recv()
        place = at.y if axis == 0 else at.x
        for e in range(8):
            z3[e, axis] = (z2[axis, place, e] + z2r[axis, 1, e]) + (z2r[axis, 2, e] + z2r[axis, 3, e])

    def p3(r):
        to = at.gy(r)
        return remote(z3.at[to], z3r.at[r], s_p3.at[r], r_p3.at[r], j, to)

    for r in (4, 3, 5, 2, 6, 1, 7):
        send(p3(r))
    collect(3)

    lane = lax.broadcasted_iota(jnp.int32, (16, 128), 1)
    for t in range(16):
        here = pl.ds(128 * (t % 8), 128)
        real = part[d, t // 8, 0:16, here]
        imag = part[d, t // 8, 16:32, here]
        a_send[2 * t] = jnp.where(lane < 64, real, pltpu.roll(imag, 64, 1))
        a_send[2 * t + 1] = jnp.where(lane < 64, pltpu.roll(real, 64, 1), imag)

    def spread_copy(out, into, s_sem, r_sem, r):
        gx = at.gx(r)
        return remote(out.at[gx], into.at[j], s_sem.at[r], r_sem.at[r], gx, d)

    def spread_start(*refs):
        def start(r, carry):
            spread_copy(*refs, r).start()
            return carry

        lax.fori_loop(1, 32, start, 0)
        out, into = refs[:2]
        into[j] = out[j]

        def sent(r, carry):
            spread_copy(*refs, r).wait_send()
            return carry

        pending.append(lambda: lax.fori_loop(1, 32, sent, 0))

    def spread_wait(*refs):
        def wait(r, carry):
            spread_copy(*refs, r).wait_recv()
            return carry

        lax.fori_loop(1, 32, wait, 0)

    a_refs = (a_send, a_recv, s_a, r_a)
    spread_start(*a_refs)

    loads[5].wait()

    def split_weight(k, carry):
        here = pl.ds(pl.multiple_of(k * 256, 256), 256)
        high, low = split(w[here])
        w_high[here] = high
        w_low[here] = low
        return carry

    lax.fori_loop(0, 16, split_weight, 0)

    for r in range(1, 8):
        p3(r).wait_recv()
    stack = []
    for axis in range(2):
        total = z3[d, axis]
        for r in range(1, 8):
            total = total + z3r[r, axis]
        stack.append(total.reshape(32, 128))

    loads[4].wait()
    spread_wait(*a_refs)
    turned = [quarters([a_recv[4 * tile + v] for v in range(4)]) for tile in range(8)]
    rows = jnp.concatenate(
        [jnp.concatenate([turned[tile][k] for tile in range(8)], axis=1) for k in range(4)], axis=0
    )
    both = dot3(split(rows), (xaf[0], xaf[1]), NN)
    for half in range(2):
        real = both[16 * half : 16 * half + 16]
        imag = both[32 + 16 * half : 32 + 16 * half + 16]
        stack.append(real[:, :128] + imag[:, 128:])
        stack.append(imag[:, :128] - real[:, 128:])
    modes = jnp.concatenate(stack, axis=0).T
    for owner in range(32):
        m_send[owner] = modes[4 * owner : 4 * owner + 4]

    m_refs = (m_send, m_recv, s_m, r_m)
    spread_start(*m_refs)
    spread_wait(*m_refs)

    held = jnp.concatenate([m_recv[:, kx, :] for kx in range(4)], axis=0).T
    lane16 = lax.broadcasted_iota(jnp.int32, (16, 128), 1)
    quarter = lane16 // 32
    ky_of = lax.broadcasted_iota(jnp.int32, (64, 128), 0) % 16
    ky_lane = lax.broadcasted_iota(jnp.int32, (64, 128), 1) // 64
    sign = jnp.where(lane16 < 64, -1.0, 1.0)
    for kx in range(4):
        rows = []
        for sample in range(2):
            for ri in range(2):
                base = 64 * (1 - sample) + 16 * ri
                low, high = held[base : base + 16], held[base + 32 : base + 48]
                moved = []
                for v in range(4):
                    shift = (32 * (v - kx)) % 128
                    source = low if v % 2 == 0 else high
                    moved.append(source if shift == 0 else pltpu.roll(source, shift, 1))
                rows.append(
                    jnp.where(
                        quarter < 2,
                        jnp.where(quarter == 0, moved[0], moved[1]),
                        jnp.where(quarter == 2, moved[2], moved[3]),
                    )
                )
        stacked = jnp.concatenate(rows, axis=0)
        top = stacked.astype(bf16).astype(f32)
        rest = stacked - top
        wide_top = jnp.concatenate(
            [jnp.where(ky_of == 2 * t + ky_lane, top, 0.0).astype(bf16) for t in range(8)], axis=1
        )
        wide_rest = jnp.concatenate(
            [jnp.where(ky_of == 2 * t + ky_lane, rest, 0.0).astype(bf16) for t in range(8)], axis=1
        )
        here = pl.ds(1024 * kx, 1024)
        product = dot3((wide_top, wide_rest), (w_high[here], w_low[here]), NN)
        for sample in range(2):
            from_real = product[32 * sample : 32 * sample + 16]
            from_imag = product[32 * sample + 16 : 32 * sample + 32]
            mixed[64 * sample + 16 * kx : 64 * sample + 16 * kx + 16, :] = (
                from_real + sign * pltpu.roll(from_imag, 64, 1)
            )
    turned_modes = mixed[...].T
    for k in range(4):
        n_send[:, k, :] = turned_modes[32 * k : 32 * k + 32]

    n_refs = (n_send, n_recv, s_n, r_n)
    spread_start(*n_refs)
    loads[6].wait()
    spread_wait(*n_refs)

    back = jnp.concatenate([n_recv[:, k, :] for k in range(4)], axis=0).T
    by_sample = []
    for sample in range(2):
        by_sample.append(
            quarters([back[64 * sample + 16 * v : 64 * sample + 16 * v + 16] for v in range(4)])
        )

    full = dot3(split(jnp.concatenate(by_sample[0], axis=0)), (xai[0], xai[1]), NN)
    real, imag = full[0:32], full[32:64]
    g_real = real[:, :1024] - imag[:, 1024:]
    g_imag = real[:, 1024:] + imag[:, :1024]
    for tile in range(8):
        here = slice(128 * tile, 128 * tile + 128)
        pieces = quarters(
            [g_real[0:16, here], g_real[16:32, here], g_imag[0:16, here], g_imag[16:32, here]]
        )
        for v in range(4):
            b_send[4 * tile + v] = pieces[v]
    b_refs = (b_send, b_recv, s_b, r_b)
    spread_start(*b_refs)

    for axis in range(2):
        for k in range(2):
            h3[axis, k] = by_sample[1][2 * k + axis]

    def q3(r):
        return remote(h3, h3r.at[d], s_q3.at[r], r_q3.at[r], j, at.gy(r))

    for r in (4, 3, 5, 2, 6, 1, 7):
        send(q3(r))
    h3r[d] = h3[...]

    spread_wait(*b_refs)
    for t in range(16):
        even, odd = b_recv[2 * t], b_recv[2 * t + 1]
        here = pl.ds(128 * (t % 8), 128)
        part[d, t // 8, 0:16, here] = jnp.where(lane < 64, even, pltpu.roll(odd, 64, 1))
        part[d, t // 8, 16:32, here] = jnp.where(lane < 64, pltpu.roll(even, 64, 1), odd)

    def lap(chain, s):
        direction, half, hops = CHAINS[chain]
        block = at.gy(-direction * s)
        src = part.at[block, half] if s == 0 else gather.at[block, half]
        return remote(
            src,
            gather.at[block, half],
            s_g.at[chain, s],
            r_g.at[chain, s],
            j,
            at.gy(direction),
        )

    def pass_on(s):
        for chain in range(4):
            hops = CHAINS[chain][2]
            if s < hops:
                lap(chain, s).wait_recv()
                if s + 1 < hops:
                    send(lap(chain, s + 1))

    for chain in range(4):
        send(lap(chain, 0))
    gather[d] = part[d]

    for r in range(1, 8):
        q3(r).wait_recv()

    def q2(axis, r):
        place, gx = at.across(axis, r)
        mine = at.y if axis == 0 else at.x
        return remote(
            h3r.at[:, axis], h2r.at[axis, mine], s_q2.at[axis, r], r_q2.at[axis, r], gx, d
        )

    for r in (1, 3, 2):
        for axis in range(2):
            send(q2(axis, r))
    h2r[0, at.y] = h3r[:, 0]
    h2r[1, at.x] = h3r[:, 1]

    for k in range(7, 10):
        loads[k].wait()

    def rows_of(axis, channel):
        real = jnp.concatenate([h2r[axis, channel, e, 0] for e in range(8)], axis=0)
        imag = jnp.concatenate([h2r[axis, channel, e, 1] for e in range(8)], axis=0)
        both = dot3((xi[axis, 0], xi[axis, 1]), split(jnp.concatenate([real, imag], axis=0)), NT)
        g_real = both[:256, :128] - both[256:, 128:]
        g_imag = both[256:, :128] + both[:256, 128:]
        wide = split(jnp.concatenate([g_real, g_imag], axis=1))
        out1[axis, channel] = dot3(wide, (yi[0], yi[1]), NN).reshape(8, 32, 256)

    def spec_piece(axis, chunk):
        if axis == 0:
            return spec.at[0, pl.ds(2 * chunk, 2), at.x, at.c]
        return spec.at[1, at.y, pl.ds(2 * chunk, 2), at.c]

    def q1(axis, chunk, r):
        place, core, gx = at.member(axis, r)
        return remote(
            out1.at[axis, pl.ds(2 * chunk, 2), place * 2 + core],
            spec_piece(axis, chunk),
            s_q1.at[axis, chunk, r],
            r_q1.at[axis, chunk, r],
            gx,
            d,
        )

    def q1_own(axis, chunk):
        place = at.x if axis == 0 else at.y
        return pltpu.make_async_copy(
            out1.at[axis, pl.ds(2 * chunk, 2), place * 2 + at.c],
            spec_piece(axis, chunk),
            own.at[axis, 2 + chunk],
        )

    def inverse_chunk(axis, chunk):
        def one(k, carry):
            rows_of(axis, 2 * chunk + k)
            return carry

        lax.fori_loop(0, 2, one, 0)
        for r in (2, 6, 3, 7, 4, 5, 1):
            send(q1(axis, chunk, r))
        q1_own(axis, chunk).start()

    for k in range(2):
        halo_row(k).wait_recv()
        halo_col(k).wait_recv()
    loads[12].wait()
    loads[13].wait()
    lax.fori_loop(0, 6, stencil, 0)
    pass_on(0)
    for axis in range(2):
        for r in range(1, 4):
            q2(axis, r).wait_recv()
    for axis in range(2):
        inverse_chunk(axis, 0)
    for axis in range(2):
        inverse_chunk(axis, 1)
    pass_on(1)
    lax.fori_loop(6, 16, stencil, 0)

    def inverse_columns(half, offsets):
        blocks = [at.gy(offset) for offset in offsets]
        table = tuple(jnp.concatenate([yia[k, e] for e in blocks], axis=0) for k in range(2))

        def one(k, carry):
            lanes = pl.ds(pl.multiple_of(128 * k, 128), 128)
            modes = jnp.concatenate([gather[e, half, :, lanes] for e in blocks], axis=0)
            both = dot3(split(modes), table, TN)
            first_channel = 2 * (8 * half + k)
            for n, channel in enumerate((0, 32, 1, 33)):
                u[first_channel + channel] = u[first_channel + channel] + both[32 * n : 32 * n + 32]
            return carry

        lax.fori_loop(0, 8, one, 0)

    for half in range(2):
        inverse_columns(half, (0, -1, 1, -2, 2))
    pass_on(2)

    def put(first_channel, count, k):
        copy = pltpu.make_async_copy(
            u.at[pl.ds(first_channel, count)], result.at[pl.ds(first_channel, count)], done.at[k]
        )
        copy.start()
        pending.append(copy.wait)

    for axis in range(2):
        for chunk in range(2):
            for r in range(1, 8):
                q1(axis, chunk, r).wait_recv()
            q1_own(axis, chunk).wait()

        def add(k, carry):
            here = pl.ds(64 + 32 * axis + 8 * k, 8)
            u[here] = u[here] + spec[axis, k].reshape(8, 32, 256)
            return carry

        lax.fori_loop(0, 4, add, 0)
        put(64 + 32 * axis, 32, axis)
    pass_on(3)
    for half in range(2):
        inverse_columns(half, (-3, 3, 4))
        put(16 * half, 16, 2 + 2 * half)
        put(32 + 16 * half, 16, 3 + 2 * half)
    finish()


def spectral_call(grid_field, coefficient, spectral_weight, local_weight, consts):
    dma = pltpu.SemaphoreType.DMA
    vmem = pltpu.VMEM
    scratch = [
        vmem((2, 2, 256, 256), bf16),
        vmem((2, 2, 512, 128), bf16),
        vmem((2, 256, 256), bf16),
        vmem((2, 256, 256), bf16),
        vmem((2, 8, 32, 256), bf16),
        vmem((2, 1024, 256), bf16),
        vmem((2, 128, 2048), bf16),
        vmem((4096, 128), f32),
        vmem((4096, 128), bf16),
        vmem((4096, 128), bf16),
        vmem((2, 512, 512), bf16),
        vmem((64, 64), f32),
        vmem((32, 256), f32),
        vmem((128, 32, 256), f32),
        vmem((128, 32, 256), f32),
        vmem((2, 128, 256), f32),
        vmem((2, 128, 256), f32),
        vmem((2, 16, 1, 256), f32),
        vmem((2, 16, 1, 256), f32),
        vmem((8, 2, 32, 1024), f32),
        vmem((4, 4, 32, 1024), f32),
        vmem((2, 4, 8, 32, 256), f32),
        vmem((2, 4, 8, 2, 16, 128), f32),
        vmem((2, 4, 8, 2, 16, 128), f32),
        vmem((8, 2, 2, 16, 128), f32),
        vmem((8, 2, 2, 16, 128), f32),
        vmem((32, 16, 128), f32),
        vmem((32, 16, 128), f32),
        vmem((32, 4, 128), f32),
        vmem((32, 4, 128), f32),
        vmem((32, 4, 128), f32),
        vmem((32, 4, 128), f32),
        vmem((128, 128), f32),
        vmem((32, 16, 128), f32),
        vmem((32, 16, 128), f32),
        vmem((2, 2, 16, 128), f32),
        vmem((8, 2, 2, 16, 128), f32),
        vmem((2, 4, 8, 2, 16, 128), f32),
        vmem((2, 4, 8, 32, 256), f32),
        vmem((8, 2, 32, 1024), f32),
        vmem((2, 4, 4, 2, 32, 256), f32),
        dma((14,)),
        dma((2, 2, 8)),
        dma((2, 2, 8)),
        dma((2, 4)),
        dma((2, 4)),
        dma((8,)),
        dma((8,)),
        dma((4, 4)),
        dma((4, 4)),
        *[dma((32,)) for _ in range(8)],
        dma((4, 4)),
        dma((4, 4)),
        dma((8,)),
        dma((8,)),
        dma((2, 4)),
        dma((2, 4)),
        dma((2, 2, 8)),
        dma((2, 2, 8)),
        *[dma((2,)) for _ in range(4)],
        dma((2, 4)),
        dma((6,)),
    ]
    hbm = pl.BlockSpec(memory_space=pl.ANY)
    return pl.pallas_call(
        spectral_kernel,
        out_shape=jax.ShapeDtypeStruct((128, 32, 256), f32),
        in_specs=[hbm] * 12,
        out_specs=hbm,
        scratch_shapes=scratch,
        compiler_params=pltpu.CompilerParams(
            collective_id=0, has_side_effects=True, vmem_limit_bytes=56 << 20
        ),
        name="spectral",
    )(
        grid_field.reshape(2, 2, 4, 4, 2, 32, 256),
        grid_field.reshape(128, 32, 256),
        spectral_weight.reshape(4096, 128),
        local_weight,
        coefficient,
        *consts,
    )


def kernel_only(consts, grid_field, coefficient, spectral_weight, local_weight):
    consts = [jnp.asarray(c) for c in consts]
    return spectral_call(grid_field, coefficient, spectral_weight, local_weight, consts)


def shards(consts, *arguments):
    return jax.nn.gelu(kernel_only(consts, *arguments).reshape(2, 64, 32, 256))


def solution(mesh):
    consts = tables()
    placed = (P(None, None, "gx", "gy"), P("gx", "gy"), P("gx", "gy", None, None), P())
    return jax.shard_map(
        functools.partial(shards, consts),
        mesh=mesh,
        in_specs=placed,
        out_specs=P(None, None, "gx", "gy"),
        check_vma=False,
    )
```

```python
import functools
import math

import jax
import jax.numpy as jnp
import ml_dtypes
import numpy as np
from jax import lax
from jax.experimental import pallas as pl
from jax.experimental.pallas import tpu as pltpu
from jax.sharding import PartitionSpec as P

MESH = pl.DeviceIdType.MESH
MX = 128
MY = 128
NX = 1024
NY = 2048
f32 = jnp.float32
bf16 = jnp.bfloat16


def halves(table):
    table = np.asarray(table, np.float64)
    high = table.astype(np.float32).astype(ml_dtypes.bfloat16)
    low = (table - high.astype(np.float64)).astype(np.float32).astype(ml_dtypes.bfloat16)
    return np.stack([high, low], axis=-3)


def angles(position, frequency, period):
    return (np.outer(position, frequency) % period) * (2.0 * math.pi / period)


def x_frequency():
    k = np.arange(MX)
    return np.where(k < MX // 2, k, k - MX + NX)


def group_rows(axis, place):
    y, x, c, r = np.meshgrid(np.arange(4), np.arange(4), np.arange(2), np.arange(32), indexing="ij")
    row = ((y * 4 + x) * 2 + c) * 32 + r
    return (row[place] if axis == 0 else row[:, place]).reshape(-1)


def tables():
    fx = x_frequency()
    spread = (np.arange(128) % 32) * 4 + np.arange(128) // 32
    x_fwd, x_inv = [], []
    for axis in (0, 1):
        for place in range(4):
            angle = angles(group_rows(axis, place), fx, NX)
            x_fwd.append(np.concatenate([np.cos(angle).T, np.sin(angle).T], 0))
            x_inv.append(np.concatenate([np.cos(angle)[:, spread], np.sin(angle)[:, spread]], 0))
    y_fwd, y_inv_a, y_inv_b = [], [], []
    weight = np.where(np.arange(MY) == 0, 1.0, 2.0) / float(NX * NY)
    for place in range(8):
        angle = angles(place * 256 + np.arange(256), np.arange(MY), NY).T
        cosine, sine = np.cos(angle), np.sin(angle)
        y_fwd.append(
            np.stack([cosine.reshape(8, 16, 256), -sine.reshape(8, 16, 256)], 1).reshape(256, 256)
        )
        cosine, sine = cosine * weight[:, None], -sine * weight[:, None]
        y_inv_a.append(
            np.stack([cosine.reshape(8, 16, 256), sine.reshape(8, 16, 256)], 1).reshape(256, 256)
        )
        y_inv_b.append(np.concatenate([cosine, sine], 0))
    angle = angles(np.arange(NX), fx, NX)
    x_all_fwd = np.concatenate([np.cos(angle), np.sin(angle)], 1)
    x_all_inv = np.concatenate([np.cos(angle)[:, spread].T, np.sin(angle)[:, spread].T], 1)
    return [
        halves(np.stack(x_fwd)),
        halves(np.stack(x_inv)),
        halves(np.stack(y_fwd)),
        halves(np.stack(y_inv_b)),
        halves(x_all_fwd),
        halves(x_all_inv),
        halves(np.stack(y_inv_a)).reshape(8, 2, 8, 32, 256),
    ]


def split(value):
    high = value.astype(bf16)
    return high, (value - high.astype(f32)).astype(bf16)


def dot(a, b, dims):
    return lax.dot_general(a, b, (dims, ((), ())), preferred_element_type=f32)


NN = ((1,), (0,))
NT = ((1,), (1,))
TN = ((0,), (0,))


def dot3(a, b, dims):
    left = jnp.concatenate([a[0], a[1], a[0]], axis=dims[0][0])
    right = jnp.concatenate([b[0], b[0], b[1]], axis=dims[1][0])
    return dot(left, right, dims)


def quarters(blocks):
    rows = blocks[0].shape[0]
    lane = lax.broadcasted_iota(jnp.int32, (rows, 128), 1) // 32
    out = []
    for k in range(4):
        result = blocks[k] if k == 0 else None
        for v in range(4):
            shift = (32 * (v - k)) % 128
            moved = blocks[v] if shift == 0 else pltpu.roll(blocks[v], shift, 1)
            result = moved if v == 0 else jnp.where(lane == v, moved, result)
        out.append(result)
    return out


class Place:
    def __init__(self):
        self.j = lax.axis_index("gx")
        self.d = lax.axis_index("gy")
        self.y = self.j // 8
        self.x = (self.j // 2) % 4
        self.c = self.j % 2
        self.ys = [self.y] + [(self.y + k) % 4 for k in range(1, 4)]
        self.xs = [self.x] + [(self.x + k) % 4 for k in range(1, 4)]
        self.cs = [self.c, 1 - self.c]
        self.ds = [self.d] + [(self.d + k) % 8 for k in range(1, 8)]

    def gx(self, r):
        return self.ys[r // 8] * 8 + self.xs[(r // 2) % 4] * 2 + self.cs[r % 2]

    def member(self, axis, r):
        core = self.cs[r % 2]
        if axis == 0:
            place = self.xs[r // 2]
            return place, core, self.y * 8 + place * 2 + core
        place = self.ys[r // 2]
        return place, core, place * 8 + self.x * 2 + core

    def across(self, axis, r):
        if axis == 0:
            place = self.ys[r % 4]
            return place, place * 8 + self.x * 2 + self.c
        place = self.xs[r % 4]
        return place, self.y * 8 + place * 2 + self.c

    def gy(self, r):
        return self.ds[r % 8]


CHAINS = ((1, 0, 4), (-1, 1, 4), (-1, 0, 3), (1, 1, 3))


def spectral_kernel(
    grid,
    flat,
    weight,
    local_weight,
    coefficient,
    t_xf,
    t_xi,
    t_yf,
    t_yi,
    t_xaf,
    t_xai,
    t_yia,
    result,
    xf,
    xi,
    yf,
    yi,
    yia,
    xaf,
    xai,
    w,
    w_high,
    w_low,
    wide,
    lw,
    coef,
    g,
    u,
    row_send,
    row_recv,
    col_send,
    col_recv,
    part,
    ring,
    first,
    z2,
    z2r,
    z3,
    z3r,
    a_send,
    a_recv,
    m_send,
    m_recv,
    n_send,
    n_recv,
    b_send,
    b_recv,
    h3,
    h3r,
    h2r,
    out1,
    gather,
    spec,
    load,
    s_p1,
    r_p1,
    s_p2,
    r_p2,
    s_p3,
    r_p3,
    s_ring,
    r_ring,
    s_a,
    r_a,
    s_m,
    r_m,
    s_n,
    r_n,
    s_b,
    r_b,
    s_g,
    r_g,
    s_q3,
    r_q3,
    s_q2,
    r_q2,
    s_q1,
    r_q1,
    s_row,
    r_row,
    s_col,
    r_col,
    own,
    done,
):
    at = Place()
    j, d = at.j, at.d

    def remote(src, dst, send, recv, gx, gy):
        return pltpu.make_async_remote_copy(
            src_ref=src, dst_ref=dst, send_sem=send, recv_sem=recv, device_id=(gx, gy), device_id_type=MESH
        )

    loads = [
        pltpu.make_async_copy(flat.at[pl.ds(0, 64)], g.at[pl.ds(0, 64)], load.at[0]),
        pltpu.make_async_copy(t_yf.at[d], yf, load.at[1]),
        pltpu.make_async_copy(t_xf.at[at.y], xf.at[0], load.at[2]),
        pltpu.make_async_copy(t_xf.at[4 + at.x], xf.at[1], load.at[3]),
        pltpu.make_async_copy(t_xaf, xaf, load.at[4]),
        pltpu.make_async_copy(weight, w, load.at[5]),
        pltpu.make_async_copy(t_xai, xai, load.at[6]),
        pltpu.make_async_copy(t_xi.at[at.y], xi.at[0], load.at[7]),
        pltpu.make_async_copy(t_xi.at[4 + at.x], xi.at[1], load.at[8]),
        pltpu.make_async_copy(t_yi.at[d], yi, load.at[9]),
        pltpu.make_async_copy(local_weight, lw, load.at[10]),
        pltpu.make_async_copy(flat.at[pl.ds(64, 64)], g.at[pl.ds(64, 64)], load.at[11]),
        pltpu.make_async_copy(coefficient, coef, load.at[12]),
        pltpu.make_async_copy(t_yia.at[d], yia, load.at[13]),
    ]
    for k in (0, 1):
        loads[k].start()

    pending = []

    def send(copy, alone=True):
        copy.start()
        if alone:
            pending.append(copy.wait_send)

    def bytes_of(ref, sem):
        return pltpu.make_async_copy(ref, ref, sem)

    def drain():
        for wait in pending:
            wait()
        pending.clear()

    barrier = pltpu.get_barrier_semaphore()

    for r in range(1, 32):
        pl.semaphore_signal(barrier, inc=1, device_id=(at.gx(r), d), device_id_type=MESH)
    for r in range(1, 8):
        pl.semaphore_signal(barrier, inc=1, device_id=(j, at.gy(r)), device_id_type=MESH)
    pl.semaphore_wait(barrier, 31 + 7)

    FAR_FIRST = (2, 6, 3, 7, 4, 5, 1)

    def grid_piece(axis, r, place, core):
        if axis == 0:
            return grid.at[1, 0, at.ys[r], place, core]
        return grid.at[1, 1, place, at.xs[r], core]

    def p1(axis, r, m):
        place, core, gx = at.member(axis, m)
        mine = (at.x if axis == 0 else at.y) * 2 + at.c
        return remote(
            grid_piece(axis, r, place, core),
            first.at[axis, at.across(axis, r)[0], mine],
            s_p1.at[axis],
            r_p1.at[axis, r],
            gx,
            d,
        )

    def p1_own(axis, r):
        place = at.x if axis == 0 else at.y
        return pltpu.make_async_copy(
            grid_piece(axis, r, place, at.c),
            first.at[axis, at.across(axis, r)[0], place * 2 + at.c],
            own.at[axis, r],
        )

    def p1_start(r):
        for m in FAR_FIRST:
            for axis in range(2):
                send(p1(axis, r, m), alone=False)
        for axis in range(2):
            p1_own(axis, r).start()

    p1_start(2)

    loads[0].wait()
    loads[1].wait()

    def columns(half, carry):
        for k in range(4):
            t = half * 8 + 2 * k
            rows = []
            for tile in range(2):
                own_of = t + tile
                for core in range(2):
                    for low in range(2):
                        rows.append(g[2 * own_of + core + 32 * low])
            block = split(jnp.concatenate(rows, axis=0))
            result = dot3((yf[0], yf[1]), block, NT)
            for e in range(8):
                part[e, half, :, 256 * k : 256 * k + 256] = result[32 * e : 32 * e + 32]
        return carry

    def hop(chain, s, piece):
        direction, half, hops = CHAINS[chain]
        to = at.gy(direction * (hops - s))
        return remote(
            part.at[to, half, pl.ds(16 * piece, 16)],
            ring.at[chain, s, pl.ds(16 * piece, 16)],
            s_ring.at[0],
            r_ring.at[chain, s, piece],
            j,
            at.gy(direction),
        )

    def collect(s):
        for piece in range(2):
            for chain in range(4):
                direction, half, hops = CHAINS[chain]
                if s < hops:
                    hop(chain, s, piece).wait_recv()
                    to = at.gy(direction * (hops - 1 - s))
                    rows = slice(16 * piece, 16 * piece + 16)
                    part[to, half, rows] = part[to, half, rows] + ring[chain, s, rows]
                    if s + 1 < hops:
                        send(hop(chain, s + 1, piece), alone=False)

    columns(0, 0)
    for piece in range(2):
        for chain in (0, 2):
            send(hop(chain, 0, piece), alone=False)
    columns(1, 0)
    for piece in range(2):
        for chain in (1, 3):
            send(hop(chain, 0, piece), alone=False)

    for r in (1, 3, 0):
        p1_start(r)
    for k in (2, 3, 4, 5, 10, 11, 12, 6, 13, 9, 7, 8):
        loads[k].start()

    def halo_row(k):
        to = (j + 31 + 2 * k) % 32
        return remote(row_send.at[k], row_recv.at[k], s_row.at[k], r_row.at[k], to, d)

    def halo_col(k):
        return remote(
            col_send.at[k], col_recv.at[k], s_col.at[k], r_col.at[k], j, at.gy(2 * k - 1)
        )

    def halos():
        for k in range(2):
            row_send[k] = g[:, 31 * k, :]
            send(halo_row(k))
        edge = lax.broadcasted_iota(jnp.int32, (16, 256), 0) * 255
        pick = jnp.where(lax.broadcasted_iota(jnp.int32, (16, 256), 1) == edge, 1.0, 0.0).astype(bf16)

        def edges(k, carry):
            high, low = split(g[pl.ds(8 * k, 8)].reshape(256, 256))
            found = dot(pick, high, NT) + dot(pick, low, NT)
            col_send[0, k] = found[0:1]
            col_send[1, k] = found[1:2]
            return carry

        lax.fori_loop(0, 16, edges, 0)
        for k in range(2):
            send(halo_col(k))

    def widen():
        loads[10].wait()
        spread_row = lax.broadcasted_iota(jnp.int32, (512, 64), 0) // 8
        repeat = jnp.where(
            spread_row == lax.broadcasted_iota(jnp.int32, (512, 64), 1), 1.0, 0.0
        ).astype(bf16)
        for part_of, piece in enumerate(split(lw[...])):
            tall = dot(repeat, piece, NN).astype(bf16)
            for k in range(4):
                block = dot(tall[128 * k : 128 * k + 128], repeat, NT)
                same = (lax.broadcasted_iota(jnp.int32, (128, 512), 0) % 8) == (
                    lax.broadcasted_iota(jnp.int32, (128, 512), 1) % 8
                )
                wide[part_of, 128 * k : 128 * k + 128, :] = jnp.where(same, block, 0.0).astype(bf16)

    def pointwise(k, carry):
        sample, rest = k // 4, k % 4
        first_row = pl.multiple_of(8 * rest, 8)
        block = split(g[pl.ds(64 * sample, 64), pl.ds(first_row, 8), :].reshape(512, 256))
        for half in range(2):
            mine = (
                wide[0, 256 * half : 256 * half + 256],
                wide[1, 256 * half : 256 * half + 256],
            )
            u[pl.ds(64 * sample + 32 * half, 32), pl.ds(first_row, 8), :] = dot3(
                mine, block, NN
            ).reshape(32, 8, 256)
        return carry

    row_of = lax.broadcasted_iota(jnp.int32, (8, 32, 256), 1)
    lane_of = lax.broadcasted_iota(jnp.int32, (256, 256), 1)

    def stencil(k, carry):
        here = pl.ds(8 * k, 8)
        block = g[here]
        square = block.reshape(256, 256)
        has_up = jnp.where(j > 0, 1.0, 0.0)
        has_down = jnp.where(j < 31, 1.0, 0.0)
        has_left = jnp.where(d > 0, 1.0, 0.0)
        has_right = jnp.where(d < 7, 1.0, 0.0)
        up = pltpu.roll(square, 1, 0).reshape(8, 32, 256)
        down = pltpu.roll(square, 255, 0).reshape(8, 32, 256)
        above = (row_recv[1, here] * has_up)[:, None, :]
        below = (row_recv[0, here] * has_down)[:, None, :]
        up = jnp.where(row_of == 0, jnp.broadcast_to(above, up.shape), up)
        down = jnp.where(row_of == 31, jnp.broadcast_to(below, up.shape), down)
        sides = jnp.concatenate(
            [
                col_recv[1, k] * has_left,
                col_recv[0, k] * has_right,
                jnp.zeros((6, 256), f32),
            ],
            axis=0,
        ).T
        left = jnp.where(lane_of == 0, sides[:, 0:1], pltpu.roll(square, 1, 1))
        right = jnp.where(lane_of == 255, sides[:, 1:2], pltpu.roll(square, 255, 1))
        beside = (up + down) + (left + right).reshape(8, 32, 256)
        u[here] = u[here] + coef[...][None] * (block - 0.25 * beside)
        return carry

    loads[2].wait()
    loads[3].wait()

    def modes_of(axis, channel):
        block = split(first[axis, channel].reshape(256, 256))
        rows = split(dot3((xf[axis, 0], xf[axis, 1]), block, NN))
        both = dot3((yf[0], yf[1]), rows, NT)
        for e in range(8):
            cos_y = both[32 * e : 32 * e + 16]
            sin_y = both[32 * e + 16 : 32 * e + 32]
            z2[axis, channel, e, 0] = cos_y[:, :128] + sin_y[:, 128:]
            z2[axis, channel, e, 1] = sin_y[:, :128] - cos_y[:, 128:]

    def p2(axis, r):
        place, gx = at.across(axis, r)
        return remote(
            z2.at[axis, place], z2r.at[axis, r], s_p2.at[axis, r], r_p2.at[axis, r], gx, d
        )

    def forward_channel(r):
        for axis in range(2):
            bytes_of(first.at[axis, at.across(axis, r)[0], pl.ds(0, 7)], r_p1.at[axis, r]).wait()
            p1_own(axis, r).wait()
            modes_of(axis, at.across(axis, r)[0])
            if r:
                send(p2(axis, r))

    widen()
    lax.fori_loop(0, 1, pointwise, 0)
    forward_channel(2)
    lax.fori_loop(1, 2, pointwise, 0)
    forward_channel(1)
    collect(0)
    forward_channel(3)
    lax.fori_loop(2, 4, pointwise, 0)
    loads[11].wait()
    forward_channel(0)
    lax.fori_loop(4, 6, pointwise, 0)
    collect(1)

    for axis in range(2):
        for r in range(1, 4):
            p2(axis, r).wait_recv()
        place = at.y if axis == 0 else at.x
        for e in range(8):
            z3[e, axis] = (z2[axis, place, e] + z2r[axis, 1, e]) + (z2r[axis, 2, e] + z2r[axis, 3, e])

    def p3(chain, s):
        direction, axis, hops = CHAINS[chain]
        to = at.gy(direction * (hops - s))
        return remote(
            z3.at[to, axis], z3r.at[chain, s], s_p3.at[chain, s], r_p3.at[chain, s], j, at.gy(direction)
        )

    def collect_modes(s):
        for chain in range(4):
            direction, axis, hops = CHAINS[chain]
            if s < hops:
                p3(chain, s).wait_recv()
                to = at.gy(direction * (hops - 1 - s))
                z3[to, axis] = z3[to, axis] + z3r[chain, s]
                if s + 1 < hops:
                    send(p3(chain, s + 1))

    for chain in range(4):
        send(p3(chain, 0))
    halos()
    collect_modes(0)
    collect(2)
    lax.fori_loop(6, 8, pointwise, 0)
    collect_modes(1)
    for k in range(2):
        halo_row(k).wait_recv()
        halo_col(k).wait_recv()
    loads[12].wait()
    lax.fori_loop(0, 4, stencil, 0)
    collect_modes(2)
    lax.fori_loop(4, 8, stencil, 0)
    collect(3)

    lane = lax.broadcasted_iota(jnp.int32, (16, 128), 1)
    for t in range(16):
        here = pl.ds(128 * (t % 8), 128)
        real = part[d, t // 8, 0:16, here]
        imag = part[d, t // 8, 16:32, here]
        a_send[2 * t] = jnp.where(lane < 64, real, pltpu.roll(imag, 64, 1))
        a_send[2 * t + 1] = jnp.where(lane < 64, pltpu.roll(real, 64, 1), imag)

    def spread_copy(out, into, s_sem, r_sem, r):
        gx = at.gx(r)
        return remote(out.at[gx], into.at[j], s_sem.at[0], r_sem.at[0], gx, d)

    def all_of(ref, sem):
        return pltpu.make_async_copy(ref.at[pl.ds(0, 31)], ref.at[pl.ds(0, 31)], sem.at[0])

    def spread_start(out, into, s_sem, r_sem):
        for r in range(1, 32):
            spread_copy(out, into, s_sem, r_sem, 32 - r).start()
        into[j] = out[j]
        pending.append(all_of(out, s_sem).wait)

    def spread_wait(out, into, s_sem, r_sem):
        all_of(into, r_sem).wait()

    a_refs = (a_send, a_recv, s_a, r_a)
    spread_start(*a_refs)

    loads[5].wait()

    def split_weight(k, carry):
        here = pl.ds(pl.multiple_of(k * 256, 256), 256)
        high, low = split(w[here])
        w_high[here] = high
        w_low[here] = low
        return carry

    lax.fori_loop(0, 16, split_weight, 0)

    def to_owners(sample, stack):
        modes = jnp.concatenate(stack + [jnp.zeros((64, 128), f32)], axis=0).T
        for owner in range(32):
            m_send[sample, owner] = modes[4 * owner : 4 * owner + 4]
        spread_start(*m_refs[sample])

    m_refs, n_refs = (
        [tuple(ref.at[sample] for ref in refs) for sample in range(2)]
        for refs in ((m_send, m_recv, s_m, r_m), (n_send, n_recv, s_n, r_n))
    )

    collect_modes(3)
    to_owners(1, [z3[d, axis].reshape(32, 128) for axis in range(2)])

    loads[4].wait()
    spread_wait(*a_refs)
    turned = [quarters([a_recv[4 * tile + v] for v in range(4)]) for tile in range(8)]
    rows = jnp.concatenate(
        [jnp.concatenate([turned[tile][k] for tile in range(8)], axis=1) for k in range(4)], axis=0
    )
    both = dot3(split(rows), (xaf[0], xaf[1]), NN)
    stack = []
    for half in range(2):
        real = both[16 * half : 16 * half + 16]
        imag = both[32 + 16 * half : 32 + 16 * half + 16]
        stack.append(real[:, :128] + imag[:, 128:])
        stack.append(imag[:, :128] - real[:, 128:])
    to_owners(0, stack)

    lane16 = lax.broadcasted_iota(jnp.int32, (16, 128), 1)
    quarter = lane16 // 32
    ky_of = lax.broadcasted_iota(jnp.int32, (32, 128), 0) % 16
    ky_lane = lax.broadcasted_iota(jnp.int32, (32, 128), 1) // 64
    sign = jnp.where(lane16 < 64, -1.0, 1.0)

    def mix(sample):
        spread_wait(*m_refs[sample])
        held = jnp.concatenate([m_recv[sample, :, kx, :] for kx in range(4)], axis=0).T
        mixed = []
        for kx in range(4):
            rows = []
            for ri in range(2):
                low, high = held[16 * ri : 16 * ri + 16], held[32 + 16 * ri : 48 + 16 * ri]
                moved = []
                for v in range(4):
                    shift = (32 * (v - kx)) % 128
                    source = low if v % 2 == 0 else high
                    moved.append(source if shift == 0 else pltpu.roll(source, shift, 1))
                rows.append(
                    jnp.where(
                        quarter < 2,
                        jnp.where(quarter == 0, moved[0], moved[1]),
                        jnp.where(quarter == 2, moved[2], moved[3]),
                    )
                )
            stacked = jnp.concatenate(rows, axis=0)
            top = stacked.astype(bf16).astype(f32)
            rest = stacked - top
            wide_top, wide_rest = (
                jnp.concatenate(
                    [jnp.where(ky_of == 2 * t + ky_lane, x, 0.0).astype(bf16) for t in range(8)], axis=1
                )
                for x in (top, rest)
            )
            here = pl.ds(1024 * kx, 1024)
            product = dot3((wide_top, wide_rest), (w_high[here], w_low[here]), NN)
            mixed.append(product[0:16] + sign * pltpu.roll(product[16:32], 64, 1))
        mixed.append(jnp.zeros((64, 128), f32))
        turned_modes = jnp.concatenate(mixed, axis=0).T
        for k in range(4):
            n_send[sample, :, k, :] = turned_modes[32 * k : 32 * k + 32]
        spread_start(*n_refs[sample])

    def unmix(sample):
        spread_wait(*n_refs[sample])
        back = jnp.concatenate([n_recv[sample, :, k, :] for k in range(4)], axis=0).T
        return quarters([back[16 * v : 16 * v + 16] for v in range(4)])

    mix(1)
    lax.fori_loop(8, 11, stencil, 0)
    mix(0)
    by_sample = [None, unmix(1)]

    for axis in range(2):
        for k in range(2):
            h3[axis, k] = by_sample[1][2 * k + axis]

    def q3(r):
        return remote(h3, h3r.at[d], s_q3.at[r], r_q3.at[r], j, at.gy(r))

    for r in (4, 3, 5, 2, 6, 1, 7):
        send(q3(r))
    h3r[d] = h3[...]

    lax.fori_loop(11, 14, stencil, 0)
    drain()
    for axis in range(2):
        bytes_of(first.at[axis, :, pl.ds(0, 7)], s_p1.at[axis]).wait()
    bytes_of(ring.at[pl.ds(0, 3)], s_ring.at[0]).wait()
    bytes_of(ring.at[3, pl.ds(0, 2)], s_ring.at[0]).wait()
    loads[6].wait()
    by_sample[0] = unmix(0)

    full = dot3(split(jnp.concatenate(by_sample[0], axis=0)), (xai[0], xai[1]), NN)
    real, imag = full[0:32], full[32:64]
    g_real = real[:, :1024] - imag[:, 1024:]
    g_imag = real[:, 1024:] + imag[:, :1024]
    for tile in range(8):
        here = slice(128 * tile, 128 * tile + 128)
        pieces = quarters(
            [g_real[0:16, here], g_real[16:32, here], g_imag[0:16, here], g_imag[16:32, here]]
        )
        for v in range(4):
            b_send[4 * tile + v] = pieces[v]
    b_refs = (b_send, b_recv, s_b, r_b)
    spread_start(*b_refs)
    lax.fori_loop(14, 16, stencil, 0)

    for r in range(1, 8):
        q3(r).wait_recv()

    def q2(axis, r):
        place, gx = at.across(axis, r)
        mine = at.y if axis == 0 else at.x
        return remote(
            h3r.at[:, axis], h2r.at[axis, mine], s_q2.at[axis, r], r_q2.at[axis, r], gx, d
        )

    for r in (1, 3, 2):
        for axis in range(2):
            send(q2(axis, r))
    h2r[0, at.y] = h3r[:, 0]
    h2r[1, at.x] = h3r[:, 1]

    spread_wait(*b_refs)
    for t in range(16):
        even, odd = b_recv[2 * t], b_recv[2 * t + 1]
        here = pl.ds(128 * (t % 8), 128)
        part[d, t // 8, 0:16, here] = jnp.where(lane < 64, even, pltpu.roll(odd, 64, 1))
        part[d, t // 8, 16:32, here] = jnp.where(lane < 64, pltpu.roll(even, 64, 1), odd)

    def lap(chain, s, piece):
        direction, half, hops = CHAINS[chain]
        block = at.gy(-direction * s)
        rows = pl.ds(16 * piece, 16)
        return remote(
            (part if s == 0 else gather).at[block, half, rows],
            gather.at[block, half, rows],
            s_g.at[0],
            r_g.at[chain, s, piece],
            j,
            at.gy(direction),
        )

    def pass_on(s):
        for piece in range(2):
            for chain in range(4):
                hops = CHAINS[chain][2]
                if s < hops:
                    lap(chain, s, piece).wait_recv()
                    if s + 1 < hops:
                        send(lap(chain, s + 1, piece), alone=False)

    for piece in range(2):
        for chain in range(4):
            send(lap(chain, 0, piece), alone=False)
    gather[d] = part[d]

    for k in range(7, 10):
        loads[k].wait()

    def rows_of(axis, channel):
        real = jnp.concatenate([h2r[axis, channel, e, 0] for e in range(8)], axis=0)
        imag = jnp.concatenate([h2r[axis, channel, e, 1] for e in range(8)], axis=0)
        both = dot3((xi[axis, 0], xi[axis, 1]), split(jnp.concatenate([real, imag], axis=0)), NT)
        g_real = both[:256, :128] - both[256:, 128:]
        g_imag = both[256:, :128] + both[:256, 128:]
        wide = split(jnp.concatenate([g_real, g_imag], axis=1))
        out1[axis, channel] = dot3(wide, (yi[0], yi[1]), NN).reshape(8, 32, 256)

    def spec_piece(axis, r):
        channel = at.across(axis, 4 - r)[0]
        return spec.at[axis, channel, (at.x if axis == 0 else at.y) * 2 + at.c]

    def q1(axis, r, m):
        place, core, gx = at.member(axis, m)
        return remote(
            out1.at[axis, at.across(axis, 4 - r)[0], place * 2 + core],
            spec_piece(axis, r),
            s_q1.at[axis],
            r_q1.at[axis],
            gx,
            d,
        )

    def q1_own(axis, r):
        place = at.x if axis == 0 else at.y
        return pltpu.make_async_copy(
            out1.at[axis, at.across(axis, 4 - r)[0], place * 2 + at.c],
            spec_piece(axis, r),
            own.at[axis, r],
        )

    def inverse_channel(r):
        for axis in range(2):
            if r:
                q2(axis, r).wait_recv()
            rows_of(axis, at.across(axis, 4 - r)[0])
            for m in FAR_FIRST:
                send(q1(axis, r, m), alone=False)
            q1_own(axis, r).start()

    inverse_channel(0)
    inverse_channel(1)
    inverse_channel(3)
    pass_on(0)
    inverse_channel(2)
    loads[13].wait()
    pass_on(1)

    def inverse_columns(half, offsets, last=False):
        blocks = [at.gy(offset) for offset in offsets]
        table = tuple(jnp.concatenate([yia[k, e] for e in blocks], axis=0) for k in range(2))

        def one(k, carry):
            lanes = pl.ds(256 * k if last else pl.multiple_of(256 * k, 256), 256)
            modes = jnp.concatenate([gather[e, half, :, lanes] for e in blocks], axis=0)
            both = dot3(split(modes), table, TN)
            first_channel = 2 * (8 * half + 2 * k)
            for n, channel in enumerate((0, 32, 1, 33, 2, 34, 3, 35)):
                u[first_channel + channel] = u[first_channel + channel] + both[32 * n : 32 * n + 32]
            return carry

        if not last:
            lax.fori_loop(0, 4, one, 0)
            return
        for k in range(4):
            one(k, 0)
            for low in range(2):
                put(16 * half + 4 * k + 32 * low, 4, 2 + 8 * half + 2 * k + low)

    def put(first_channel, count, k):
        copy = pltpu.make_async_copy(
            u.at[pl.ds(first_channel, count)], result.at[pl.ds(first_channel, count)], done.at[k]
        )
        copy.start()
        pending.append(copy.wait)

    for half in range(2):
        inverse_columns(half, (0, -1, 1, -2, 2))
    pass_on(2)
    for half in range(2):
        inverse_columns(half, (-3, 3))
    for axis in range(2):
        bytes_of(spec.at[axis, :, pl.ds(0, 7)], r_q1.at[axis]).wait()
        for r in range(4):
            q1_own(axis, r).wait()

        def add(k, carry):
            if axis == 0:
                here = pl.ds(64 + 8 * k, 8)
                u[here] = u[here] + spec[0, k]
            else:
                for place in range(4):
                    here = pl.ds(96 + 8 * k + 2 * place, 2)
                    u[here] = u[here] + spec[1, place, pl.ds(2 * k, 2)]
            return carry

        lax.fori_loop(0, 4, add, 0)
        put(64 + 32 * axis, 32, axis)
    pass_on(3)
    for half in range(2):
        inverse_columns(half, (4,), last=True)
    drain()
    for axis in range(2):
        bytes_of(out1.at[axis, :, pl.ds(0, 7)], s_q1.at[axis]).wait()
    bytes_of(ring.at[pl.ds(0, 3)], s_g.at[0]).wait()
    bytes_of(ring.at[3, pl.ds(0, 2)], s_g.at[0]).wait()


def spectral_call(grid_field, coefficient, spectral_weight, local_weight, consts):
    dma = pltpu.SemaphoreType.DMA
    vmem = pltpu.VMEM
    scratch = [
        vmem((2, 2, 256, 256), bf16),
        vmem((2, 2, 512, 128), bf16),
        vmem((2, 256, 256), bf16),
        vmem((2, 256, 256), bf16),
        vmem((2, 8, 32, 256), bf16),
        vmem((2, 1024, 256), bf16),
        vmem((2, 128, 2048), bf16),
        vmem((4096, 128), f32),
        vmem((4096, 128), bf16),
        vmem((4096, 128), bf16),
        vmem((2, 512, 512), bf16),
        vmem((64, 64), f32),
        vmem((32, 256), f32),
        vmem((128, 32, 256), f32),
        vmem((128, 32, 256), f32),
        vmem((2, 128, 256), f32),
        vmem((2, 128, 256), f32),
        vmem((2, 16, 1, 256), f32),
        vmem((2, 16, 1, 256), f32),
        vmem((8, 2, 32, 1024), f32),
        vmem((4, 4, 32, 1024), f32),
        vmem((2, 4, 8, 32, 256), f32),
        vmem((2, 4, 8, 2, 16, 128), f32),
        vmem((2, 4, 8, 2, 16, 128), f32),
        vmem((8, 2, 2, 16, 128), f32),
        vmem((4, 4, 2, 16, 128), f32),
        vmem((32, 16, 128), f32),
        vmem((32, 16, 128), f32),
        vmem((2, 32, 4, 128), f32),
        vmem((2, 32, 4, 128), f32),
        vmem((2, 32, 4, 128), f32),
        vmem((2, 32, 4, 128), f32),
        vmem((32, 16, 128), f32),
        vmem((32, 16, 128), f32),
        vmem((2, 2, 16, 128), f32),
        vmem((8, 2, 2, 16, 128), f32),
        vmem((2, 4, 8, 2, 16, 128), f32),
        vmem((2, 4, 8, 32, 256), f32),
        vmem((8, 2, 32, 1024), f32),
        vmem((2, 4, 8, 32, 256), f32),
        dma((14,)),
        dma((2,)),
        dma((2, 4)),
        dma((2, 4)),
        dma((2, 4)),
        dma((4, 4)),
        dma((4, 4)),
        dma((1,)),
        dma((4, 4, 2)),
        *[dma((1,)) for _ in range(2)],
        *[dma((2, 1)) for _ in range(4)],
        *[dma((1,)) for _ in range(2)],
        dma((1,)),
        dma((4, 4, 2)),
        dma((8,)),
        dma((8,)),
        dma((2, 4)),
        dma((2, 4)),
        dma((2,)),
        dma((2,)),
        *[dma((2,)) for _ in range(4)],
        dma((2, 4)),
        dma((18,)),
    ]
    hbm = pl.BlockSpec(memory_space=pl.ANY)
    return pl.pallas_call(
        spectral_kernel,
        out_shape=jax.ShapeDtypeStruct((128, 32, 256), f32),
        in_specs=[hbm] * 12,
        out_specs=hbm,
        scratch_shapes=scratch,
        compiler_params=pltpu.CompilerParams(
            collective_id=0, has_side_effects=True, vmem_limit_bytes=56 << 20
        ),
        name="spectral",
    )(
        grid_field.reshape(2, 2, 4, 4, 2, 32, 256),
        grid_field.reshape(128, 32, 256),
        spectral_weight.reshape(4096, 128),
        local_weight,
        coefficient,
        *consts,
    )


def kernel_only(consts, grid_field, coefficient, spectral_weight, local_weight):
    consts = [jnp.asarray(c) for c in consts]
    return spectral_call(grid_field, coefficient, spectral_weight, local_weight, consts)


def shards(consts, *arguments):
    return jax.nn.gelu(kernel_only(consts, *arguments).reshape(2, 64, 32, 256))


def solution(mesh):
    consts = tables()
    placed = (P(None, None, "gx", "gy"), P("gx", "gy"), P("gx", "gy", None, None), P())
    return jax.shard_map(
        functools.partial(shards, consts),
        mesh=mesh,
        in_specs=placed,
        out_specs=P(None, None, "gx", "gy"),
        check_vma=False,
    )
```

```python
import functools
import math

import jax
import jax.numpy as jnp
import ml_dtypes
import numpy as np
from jax import lax
from jax.experimental import pallas as pl
from jax.experimental.pallas import tpu as pltpu
from jax.sharding import PartitionSpec as P

MESH = pl.DeviceIdType.MESH
MX = 128
MY = 128
NX = 1024
NY = 2048
f32 = jnp.float32
bf16 = jnp.bfloat16


def halves(table):
    table = np.asarray(table, np.float64)
    high = table.astype(np.float32).astype(ml_dtypes.bfloat16)
    low = (table - high.astype(np.float64)).astype(np.float32).astype(ml_dtypes.bfloat16)
    return np.stack([high, low], axis=-3)


def angles(position, frequency, period):
    return (np.outer(position, frequency) % period) * (2.0 * math.pi / period)


def x_frequency():
    k = np.arange(MX)
    return np.where(k < MX // 2, k, k - MX + NX)


def group_rows(axis, place):
    y, x, c, r = np.meshgrid(np.arange(4), np.arange(4), np.arange(2), np.arange(32), indexing="ij")
    row = ((y * 4 + x) * 2 + c) * 32 + r
    return (row[place] if axis == 0 else row[:, place]).reshape(-1)


def tables():
    fx = x_frequency()
    spread = (np.arange(128) % 32) * 4 + np.arange(128) // 32
    x_fwd, x_inv = [], []
    for axis in (0, 1):
        for place in range(4):
            angle = angles(group_rows(axis, place), fx, NX)
            x_fwd.append(np.concatenate([np.cos(angle).T, np.sin(angle).T], 0))
            x_inv.append(np.concatenate([np.cos(angle)[:, spread], np.sin(angle)[:, spread]], 0))
    y_fwd, y_inv_a, y_inv_b = [], [], []
    weight = np.where(np.arange(MY) == 0, 1.0, 2.0) / float(NX * NY)
    for place in range(8):
        angle = angles(place * 256 + np.arange(256), np.arange(MY), NY).T
        cosine, sine = np.cos(angle), np.sin(angle)
        y_fwd.append(
            np.stack([cosine.reshape(8, 16, 256), -sine.reshape(8, 16, 256)], 1).reshape(256, 256)
        )
        cosine, sine = cosine * weight[:, None], -sine * weight[:, None]
        y_inv_a.append(
            np.stack([cosine.reshape(8, 16, 256), sine.reshape(8, 16, 256)], 1).reshape(256, 256)
        )
        y_inv_b.append(np.concatenate([cosine, sine], 0))
    angle = angles(np.arange(NX), fx, NX)
    x_all_fwd = np.concatenate([np.cos(angle), np.sin(angle)], 1)
    x_all_inv = np.concatenate([np.cos(angle)[:, spread].T, np.sin(angle)[:, spread].T], 1)
    return [
        halves(np.stack(x_fwd)),
        halves(np.stack(x_inv)),
        halves(np.stack(y_fwd)),
        halves(np.stack(y_inv_b)),
        halves(x_all_fwd),
        halves(x_all_inv),
        halves(np.stack(y_inv_a)).reshape(8, 2, 8, 32, 256),
    ]


def split(value):
    high = value.astype(bf16)
    return high, (value - high.astype(f32)).astype(bf16)


def dot(a, b, dims):
    return lax.dot_general(a, b, (dims, ((), ())), preferred_element_type=f32)


NN = ((1,), (0,))
NT = ((1,), (1,))
TN = ((0,), (0,))


def dot3(a, b, dims):
    left = jnp.concatenate([a[0], a[1], a[0]], axis=dims[0][0])
    right = jnp.concatenate([b[0], b[0], b[1]], axis=dims[1][0])
    return dot(left, right, dims)


def quarters(blocks):
    rows = blocks[0].shape[0]
    lane = lax.broadcasted_iota(jnp.int32, (rows, 128), 1) // 32
    out = []
    for k in range(4):
        result = blocks[k] if k == 0 else None
        for v in range(4):
            shift = (32 * (v - k)) % 128
            moved = blocks[v] if shift == 0 else pltpu.roll(blocks[v], shift, 1)
            result = moved if v == 0 else jnp.where(lane == v, moved, result)
        out.append(result)
    return out


class Place:
    def __init__(self):
        self.j = lax.axis_index("gx")
        self.d = lax.axis_index("gy")
        self.y = self.j // 8
        self.x = (self.j // 2) % 4
        self.c = self.j % 2
        self.ys = [self.y] + [(self.y + k) % 4 for k in range(1, 4)]
        self.xs = [self.x] + [(self.x + k) % 4 for k in range(1, 4)]
        self.cs = [self.c, 1 - self.c]
        self.ds = [self.d] + [(self.d + k) % 8 for k in range(1, 8)]

    def gx(self, r):
        return self.ys[r // 8] * 8 + self.xs[(r // 2) % 4] * 2 + self.cs[r % 2]

    def member(self, axis, r):
        core = self.cs[r % 2]
        if axis == 0:
            place = self.xs[r // 2]
            return place, core, self.y * 8 + place * 2 + core
        place = self.ys[r // 2]
        return place, core, place * 8 + self.x * 2 + core

    def across(self, axis, r):
        if axis == 0:
            place = self.ys[r % 4]
            return place, place * 8 + self.x * 2 + self.c
        place = self.xs[r % 4]
        return place, self.y * 8 + place * 2 + self.c

    def gy(self, r):
        return self.ds[r % 8]


CHAINS = ((1, 0, 4), (-1, 1, 4), (-1, 0, 3), (1, 1, 3))


def spectral_kernel(
    grid,
    flat,
    weight,
    local_weight,
    coefficient,
    t_xf,
    t_xi,
    t_yf,
    t_yi,
    t_xaf,
    t_xai,
    t_yia,
    result,
    xf,
    xi,
    yf,
    yi,
    yia,
    xaf,
    xai,
    w,
    w_high,
    w_low,
    wide,
    lw,
    coef,
    g,
    u,
    row_send,
    row_recv,
    col_send,
    col_recv,
    part,
    ring,
    first,
    z2,
    z2r,
    z3,
    z3r,
    a_send,
    a_recv,
    m_send,
    m_recv,
    n_send,
    n_recv,
    b_send,
    b_recv,
    h3,
    h3r,
    h2r,
    out1,
    gather,
    spec,
    load,
    s_p1,
    r_p1,
    s_p2,
    r_p2,
    s_p3,
    r_p3,
    s_ring,
    r_ring,
    s_a,
    r_a,
    s_m,
    r_m,
    s_n,
    r_n,
    s_b,
    r_b,
    s_g,
    r_g,
    s_q3,
    r_q3,
    s_q2,
    r_q2,
    s_q1,
    r_q1,
    s_row,
    r_row,
    s_col,
    r_col,
    own,
    done,
):
    at = Place()
    j, d = at.j, at.d

    def remote(src, dst, send, recv, gx, gy):
        return pltpu.make_async_remote_copy(
            src_ref=src, dst_ref=dst, send_sem=send, recv_sem=recv, device_id=(gx, gy), device_id_type=MESH
        )

    loads = [
        pltpu.make_async_copy(flat.at[pl.ds(0, 64)], g.at[pl.ds(0, 64)], load.at[0]),
        pltpu.make_async_copy(t_yf.at[d], yf, load.at[1]),
        pltpu.make_async_copy(t_xf.at[at.y], xf.at[0], load.at[2]),
        pltpu.make_async_copy(t_xf.at[4 + at.x], xf.at[1], load.at[3]),
        pltpu.make_async_copy(t_xaf, xaf, load.at[4]),
        pltpu.make_async_copy(weight, w, load.at[5]),
        pltpu.make_async_copy(t_xai, xai, load.at[6]),
        pltpu.make_async_copy(t_xi.at[at.y], xi.at[0], load.at[7]),
        pltpu.make_async_copy(t_xi.at[4 + at.x], xi.at[1], load.at[8]),
        pltpu.make_async_copy(t_yi.at[d], yi, load.at[9]),
        pltpu.make_async_copy(local_weight, lw, load.at[10]),
        pltpu.make_async_copy(flat.at[pl.ds(64, 64)], g.at[pl.ds(64, 64)], load.at[11]),
        pltpu.make_async_copy(coefficient, coef, load.at[12]),
        pltpu.make_async_copy(t_yia.at[d], yia, load.at[13]),
    ]
    for k in (0, 1):
        loads[k].start()

    pending = []

    def send(copy, alone=True):
        copy.start()
        if alone:
            pending.append(copy.wait_send)

    def bytes_of(ref, sem):
        return pltpu.make_async_copy(ref, ref, sem)

    def drain():
        for wait in pending:
            wait()
        pending.clear()

    barrier = pltpu.get_barrier_semaphore()

    for r in range(1, 32):
        pl.semaphore_signal(barrier, inc=1, device_id=(at.gx(r), d), device_id_type=MESH)
    for r in range(1, 8):
        pl.semaphore_signal(barrier, inc=1, device_id=(j, at.gy(r)), device_id_type=MESH)
    pl.semaphore_wait(barrier, 31 + 7)

    FAR_FIRST = (2, 6, 3, 7, 4, 5, 1)

    def grid_piece(axis, r, place, core):
        if axis == 0:
            return grid.at[1, 0, at.ys[r], place, core]
        return grid.at[1, 1, place, at.xs[r], core]

    def p1(axis, r, m):
        place, core, gx = at.member(axis, m)
        mine = (at.x if axis == 0 else at.y) * 2 + at.c
        return remote(
            grid_piece(axis, r, place, core),
            first.at[axis, at.across(axis, r)[0], mine],
            s_p1.at[axis],
            r_p1.at[axis, r],
            gx,
            d,
        )

    def p1_own(axis, r):
        place = at.x if axis == 0 else at.y
        return pltpu.make_async_copy(
            grid_piece(axis, r, place, at.c),
            first.at[axis, at.across(axis, r)[0], place * 2 + at.c],
            own.at[axis, r],
        )

    def p1_start(r):
        for m in FAR_FIRST:
            for axis in range(2):
                send(p1(axis, r, m), alone=False)
        for axis in range(2):
            p1_own(axis, r).start()

    p1_start(2)

    loads[0].wait()
    loads[1].wait()

    def columns(half, carry):
        for k in range(4):
            t = half * 8 + 2 * k
            rows = []
            for tile in range(2):
                own_of = t + tile
                for core in range(2):
                    for low in range(2):
                        rows.append(g[2 * own_of + core + 32 * low])
            block = split(jnp.concatenate(rows, axis=0))
            result = dot3((yf[0], yf[1]), block, NT)
            for e in range(8):
                part[e, half, :, 256 * k : 256 * k + 256] = result[32 * e : 32 * e + 32]
        return carry

    def hop(chain, s, piece):
        direction, half, hops = CHAINS[chain]
        to = at.gy(direction * (hops - s))
        return remote(
            part.at[to, half, pl.ds(0, 32)],
            ring.at[chain, s, pl.ds(0, 32)],
            s_ring.at[0],
            r_ring.at[chain, s, piece],
            j,
            at.gy(direction),
        )

    def collect(s):
        for piece in range(1):
            for chain in range(4):
                direction, half, hops = CHAINS[chain]
                if s < hops:
                    hop(chain, s, piece).wait_recv()
                    to = at.gy(direction * (hops - 1 - s))
                    rows = slice(0, 32)
                    part[to, half, rows] = part[to, half, rows] + ring[chain, s, rows]
                    if s + 1 < hops:
                        send(hop(chain, s + 1, piece), alone=False)

    columns(0, 0)
    for piece in range(1):
        for chain in (0, 2):
            send(hop(chain, 0, piece), alone=False)
    columns(1, 0)
    for piece in range(1):
        for chain in (1, 3):
            send(hop(chain, 0, piece), alone=False)

    for r in (1, 3, 0):
        p1_start(r)
    for k in (2, 3, 4, 5, 10, 11, 12, 6, 13, 9, 7, 8):
        loads[k].start()

    def halo_row(k):
        to = (j + 31 + 2 * k) % 32
        return remote(row_send.at[k], row_recv.at[k], s_row.at[k], r_row.at[k], to, d)

    def halo_col(k):
        return remote(
            col_send.at[k], col_recv.at[k], s_col.at[k], r_col.at[k], j, at.gy(2 * k - 1)
        )

    def halos():
        for k in range(2):
            row_send[k] = g[:, 31 * k, :]
            send(halo_row(k))
        edge = lax.broadcasted_iota(jnp.int32, (16, 256), 0) * 255
        pick = jnp.where(lax.broadcasted_iota(jnp.int32, (16, 256), 1) == edge, 1.0, 0.0).astype(bf16)

        def edges(k, carry):
            high, low = split(g[pl.ds(8 * k, 8)].reshape(256, 256))
            found = dot(pick, high, NT) + dot(pick, low, NT)
            col_send[0, k] = found[0:1]
            col_send[1, k] = found[1:2]
            return carry

        lax.fori_loop(0, 16, edges, 0)
        for k in range(2):
            send(halo_col(k))

    def widen():
        loads[10].wait()
        spread_row = lax.broadcasted_iota(jnp.int32, (512, 64), 0) // 8
        repeat = jnp.where(
            spread_row == lax.broadcasted_iota(jnp.int32, (512, 64), 1), 1.0, 0.0
        ).astype(bf16)
        for part_of, piece in enumerate(split(lw[...])):
            tall = dot(repeat, piece, NN).astype(bf16)
            for k in range(4):
                block = dot(tall[128 * k : 128 * k + 128], repeat, NT)
                same = (lax.broadcasted_iota(jnp.int32, (128, 512), 0) % 8) == (
                    lax.broadcasted_iota(jnp.int32, (128, 512), 1) % 8
                )
                wide[part_of, 128 * k : 128 * k + 128, :] = jnp.where(same, block, 0.0).astype(bf16)

    def pointwise(k, carry):
        sample, rest = k // 4, k % 4
        first_row = pl.multiple_of(8 * rest, 8)
        block = split(g[pl.ds(64 * sample, 64), pl.ds(first_row, 8), :].reshape(512, 256))
        for half in range(2):
            mine = (
                wide[0, 256 * half : 256 * half + 256],
                wide[1, 256 * half : 256 * half + 256],
            )
            u[pl.ds(64 * sample + 32 * half, 32), pl.ds(first_row, 8), :] = dot3(
                mine, block, NN
            ).reshape(32, 8, 256)
        return carry

    row_of = lax.broadcasted_iota(jnp.int32, (8, 32, 256), 1)
    lane_of = lax.broadcasted_iota(jnp.int32, (256, 256), 1)

    def stencil(k, carry):
        here = pl.ds(8 * k, 8)
        block = g[here]
        square = block.reshape(256, 256)
        has_up = jnp.where(j > 0, 1.0, 0.0)
        has_down = jnp.where(j < 31, 1.0, 0.0)
        has_left = jnp.where(d > 0, 1.0, 0.0)
        has_right = jnp.where(d < 7, 1.0, 0.0)
        up = pltpu.roll(square, 1, 0).reshape(8, 32, 256)
        down = pltpu.roll(square, 255, 0).reshape(8, 32, 256)
        above = (row_recv[1, here] * has_up)[:, None, :]
        below = (row_recv[0, here] * has_down)[:, None, :]
        up = jnp.where(row_of == 0, jnp.broadcast_to(above, up.shape), up)
        down = jnp.where(row_of == 31, jnp.broadcast_to(below, up.shape), down)
        sides = jnp.concatenate(
            [
                col_recv[1, k] * has_left,
                col_recv[0, k] * has_right,
                jnp.zeros((6, 256), f32),
            ],
            axis=0,
        ).T
        left = jnp.where(lane_of == 0, sides[:, 0:1], pltpu.roll(square, 1, 1))
        right = jnp.where(lane_of == 255, sides[:, 1:2], pltpu.roll(square, 255, 1))
        beside = (up + down) + (left + right).reshape(8, 32, 256)
        u[here] = u[here] + coef[...][None] * (block - 0.25 * beside)
        return carry

    loads[2].wait()
    loads[3].wait()

    def modes_of(axis, channel):
        block = split(first[axis, channel].reshape(256, 256))
        rows = split(dot3((xf[axis, 0], xf[axis, 1]), block, NN))
        both = dot3((yf[0], yf[1]), rows, NT)
        for e in range(8):
            cos_y = both[32 * e : 32 * e + 16]
            sin_y = both[32 * e + 16 : 32 * e + 32]
            z2[axis, channel, e, 0] = cos_y[:, :128] + sin_y[:, 128:]
            z2[axis, channel, e, 1] = sin_y[:, :128] - cos_y[:, 128:]

    def p2(axis, r):
        place, gx = at.across(axis, r)
        return remote(
            z2.at[axis, place], z2r.at[axis, r], s_p2.at[axis, r], r_p2.at[axis, r], gx, d
        )

    def forward_channel(r):
        for axis in range(2):
            bytes_of(first.at[axis, at.across(axis, r)[0], pl.ds(0, 7)], r_p1.at[axis, r]).wait()
            p1_own(axis, r).wait()
            modes_of(axis, at.across(axis, r)[0])
            if r:
                send(p2(axis, r))

    widen()
    lax.fori_loop(0, 1, pointwise, 0)
    forward_channel(2)
    lax.fori_loop(1, 2, pointwise, 0)
    forward_channel(1)
    collect(0)
    forward_channel(3)
    lax.fori_loop(2, 4, pointwise, 0)
    loads[11].wait()
    forward_channel(0)
    lax.fori_loop(4, 6, pointwise, 0)
    collect(1)

    for axis in range(2):
        for r in range(1, 4):
            p2(axis, r).wait_recv()
        place = at.y if axis == 0 else at.x
        for e in range(8):
            z3[e, axis] = (z2[axis, place, e] + z2r[axis, 1, e]) + (z2r[axis, 2, e] + z2r[axis, 3, e])

    def p3(chain, s):
        direction, axis, hops = CHAINS[chain]
        to = at.gy(direction * (hops - s))
        return remote(
            z3.at[to, axis], z3r.at[chain, s], s_p3.at[chain, s], r_p3.at[chain, s], j, at.gy(direction)
        )

    def collect_modes(s):
        for chain in range(4):
            direction, axis, hops = CHAINS[chain]
            if s < hops:
                p3(chain, s).wait_recv()
                to = at.gy(direction * (hops - 1 - s))
                z3[to, axis] = z3[to, axis] + z3r[chain, s]
                if s + 1 < hops:
                    send(p3(chain, s + 1))

    for chain in range(4):
        send(p3(chain, 0))
    halos()
    collect_modes(0)
    collect(2)
    lax.fori_loop(6, 8, pointwise, 0)
    collect_modes(1)
    for k in range(2):
        halo_row(k).wait_recv()
        halo_col(k).wait_recv()
    loads[12].wait()
    lax.fori_loop(0, 4, stencil, 0)
    collect_modes(2)
    lax.fori_loop(4, 8, stencil, 0)
    collect(3)

    lane = lax.broadcasted_iota(jnp.int32, (16, 128), 1)
    for t in range(16):
        here = pl.ds(128 * (t % 8), 128)
        real = part[d, t // 8, 0:16, here]
        imag = part[d, t // 8, 16:32, here]
        a_send[2 * t] = jnp.where(lane < 64, real, pltpu.roll(imag, 64, 1))
        a_send[2 * t + 1] = jnp.where(lane < 64, pltpu.roll(real, 64, 1), imag)

    def spread_copy(out, into, s_sem, r_sem, r):
        gx = at.gx(r)
        return remote(out.at[gx], into.at[j], s_sem.at[0], r_sem.at[0], gx, d)

    def all_of(ref, sem):
        return pltpu.make_async_copy(ref.at[pl.ds(0, 31)], ref.at[pl.ds(0, 31)], sem.at[0])

    def spread_start(out, into, s_sem, r_sem):
        for r in range(1, 32):
            spread_copy(out, into, s_sem, r_sem, 32 - r).start()
        into[j] = out[j]
        pending.append(all_of(out, s_sem).wait)

    def spread_wait(out, into, s_sem, r_sem):
        all_of(into, r_sem).wait()

    a_refs = (a_send, a_recv, s_a, r_a)
    spread_start(*a_refs)

    loads[5].wait()

    def split_weight(k, carry):
        here = pl.ds(pl.multiple_of(k * 256, 256), 256)
        high, low = split(w[here])
        w_high[here] = high
        w_low[here] = low
        return carry

    lax.fori_loop(0, 16, split_weight, 0)

    def to_owners(sample, stack):
        modes = jnp.concatenate(stack + [jnp.zeros((64, 128), f32)], axis=0).T
        for owner in range(32):
            m_send[sample, owner] = modes[4 * owner : 4 * owner + 4]
        spread_start(*m_refs[sample])

    m_refs, n_refs = (
        [tuple(ref.at[sample] for ref in refs) for sample in range(2)]
        for refs in ((m_send, m_recv, s_m, r_m), (n_send, n_recv, s_n, r_n))
    )

    collect_modes(3)
    to_owners(1, [z3[d, axis].reshape(32, 128) for axis in range(2)])

    loads[4].wait()
    spread_wait(*a_refs)
    turned = [quarters([a_recv[4 * tile + v] for v in range(4)]) for tile in range(8)]
    rows = jnp.concatenate(
        [jnp.concatenate([turned[tile][k] for tile in range(8)], axis=1) for k in range(4)], axis=0
    )
    both = dot3(split(rows), (xaf[0], xaf[1]), NN)
    stack = []
    for half in range(2):
        real = both[16 * half : 16 * half + 16]
        imag = both[32 + 16 * half : 32 + 16 * half + 16]
        stack.append(real[:, :128] + imag[:, 128:])
        stack.append(imag[:, :128] - real[:, 128:])
    to_owners(0, stack)

    lane16 = lax.broadcasted_iota(jnp.int32, (16, 128), 1)
    quarter = lane16 // 32
    ky_of = lax.broadcasted_iota(jnp.int32, (32, 128), 0) % 16
    ky_lane = lax.broadcasted_iota(jnp.int32, (32, 128), 1) // 64
    sign = jnp.where(lane16 < 64, -1.0, 1.0)

    def mix(sample):
        spread_wait(*m_refs[sample])
        held = jnp.concatenate([m_recv[sample, :, kx, :] for kx in range(4)], axis=0).T
        mixed = []
        for kx in range(4):
            rows = []
            for ri in range(2):
                low, high = held[16 * ri : 16 * ri + 16], held[32 + 16 * ri : 48 + 16 * ri]
                moved = []
                for v in range(4):
                    shift = (32 * (v - kx)) % 128
                    source = low if v % 2 == 0 else high
                    moved.append(source if shift == 0 else pltpu.roll(source, shift, 1))
                rows.append(
                    jnp.where(
                        quarter < 2,
                        jnp.where(quarter == 0, moved[0], moved[1]),
                        jnp.where(quarter == 2, moved[2], moved[3]),
                    )
                )
            stacked = jnp.concatenate(rows, axis=0)
            top = stacked.astype(bf16).astype(f32)
            rest = stacked - top
            wide_top, wide_rest = (
                jnp.concatenate(
                    [jnp.where(ky_of == 2 * t + ky_lane, x, 0.0).astype(bf16) for t in range(8)], axis=1
                )
                for x in (top, rest)
            )
            here = pl.ds(1024 * kx, 1024)
            product = dot3((wide_top, wide_rest), (w_high[here], w_low[here]), NN)
            mixed.append(product[0:16] + sign * pltpu.roll(product[16:32], 64, 1))
        mixed.append(jnp.zeros((64, 128), f32))
        turned_modes = jnp.concatenate(mixed, axis=0).T
        for k in range(4):
            n_send[sample, :, k, :] = turned_modes[32 * k : 32 * k + 32]
        spread_start(*n_refs[sample])

    def unmix(sample):
        spread_wait(*n_refs[sample])
        back = jnp.concatenate([n_recv[sample, :, k, :] for k in range(4)], axis=0).T
        return quarters([back[16 * v : 16 * v + 16] for v in range(4)])

    mix(1)
    lax.fori_loop(8, 11, stencil, 0)
    mix(0)
    by_sample = [None, unmix(1)]

    for axis in range(2):
        for k in range(2):
            h3[axis, k] = by_sample[1][2 * k + axis]

    def q3(r):
        return remote(h3, h3r.at[d], s_q3.at[r], r_q3.at[r], j, at.gy(r))

    for r in (4, 3, 5, 2, 6, 1, 7):
        send(q3(r))
    h3r[d] = h3[...]

    lax.fori_loop(11, 14, stencil, 0)
    drain()
    for axis in range(2):
        bytes_of(first.at[axis, :, pl.ds(0, 7)], s_p1.at[axis]).wait()
    bytes_of(ring.at[pl.ds(0, 3)], s_ring.at[0]).wait()
    bytes_of(ring.at[3, pl.ds(0, 2)], s_ring.at[0]).wait()
    loads[6].wait()
    by_sample[0] = unmix(0)

    full = dot3(split(jnp.concatenate(by_sample[0], axis=0)), (xai[0], xai[1]), NN)
    real, imag = full[0:32], full[32:64]
    g_real = real[:, :1024] - imag[:, 1024:]
    g_imag = real[:, 1024:] + imag[:, :1024]
    for tile in range(8):
        here = slice(128 * tile, 128 * tile + 128)
        pieces = quarters(
            [g_real[0:16, here], g_real[16:32, here], g_imag[0:16, here], g_imag[16:32, here]]
        )
        for v in range(4):
            b_send[4 * tile + v] = pieces[v]
    b_refs = (b_send, b_recv, s_b, r_b)
    spread_start(*b_refs)
    lax.fori_loop(14, 16, stencil, 0)

    spread_wait(*b_refs)
    for t in range(16):
        even, odd = b_recv[2 * t], b_recv[2 * t + 1]
        here = pl.ds(128 * (t % 8), 128)
        part[d, t // 8, 0:16, here] = jnp.where(lane < 64, even, pltpu.roll(odd, 64, 1))
        part[d, t // 8, 16:32, here] = jnp.where(lane < 64, pltpu.roll(even, 64, 1), odd)

    def lap(chain, s, piece):
        direction, half, hops = CHAINS[chain]
        block = at.gy(-direction * s)
        rows = pl.ds(0, 32)
        return remote(
            (part if s == 0 else gather).at[block, half, rows],
            gather.at[block, half, rows],
            s_g.at[0],
            r_g.at[chain, s, piece],
            j,
            at.gy(direction),
        )

    def pass_on(s):
        for piece in range(1):
            for chain in range(4):
                hops = CHAINS[chain][2]
                if s < hops:
                    lap(chain, s, piece).wait_recv()
                    if s + 1 < hops:
                        send(lap(chain, s + 1, piece), alone=False)

    for piece in range(1):
        for chain in range(4):
            send(lap(chain, 0, piece), alone=False)
    gather[d] = part[d]

    for r in range(1, 8):
        q3(r).wait_recv()

    def q2(axis, r):
        place, gx = at.across(axis, r)
        mine = at.y if axis == 0 else at.x
        return remote(
            h3r.at[:, axis], h2r.at[axis, mine], s_q2.at[axis, r], r_q2.at[axis, r], gx, d
        )

    for r in (1, 3, 2):
        for axis in range(2):
            send(q2(axis, r))
    h2r[0, at.y] = h3r[:, 0]
    h2r[1, at.x] = h3r[:, 1]

    for k in range(7, 10):
        loads[k].wait()

    def rows_of(axis, channel):
        real = jnp.concatenate([h2r[axis, channel, e, 0] for e in range(8)], axis=0)
        imag = jnp.concatenate([h2r[axis, channel, e, 1] for e in range(8)], axis=0)
        both = dot3((xi[axis, 0], xi[axis, 1]), split(jnp.concatenate([real, imag], axis=0)), NT)
        g_real = both[:256, :128] - both[256:, 128:]
        g_imag = both[256:, :128] + both[:256, 128:]
        wide = split(jnp.concatenate([g_real, g_imag], axis=1))
        out1[axis, channel] = dot3(wide, (yi[0], yi[1]), NN).reshape(8, 32, 256)

    def spec_piece(axis, r):
        channel = at.across(axis, 4 - r)[0]
        return spec.at[axis, channel, (at.x if axis == 0 else at.y) * 2 + at.c]

    def q1(axis, r, m):
        place, core, gx = at.member(axis, m)
        return remote(
            out1.at[axis, at.across(axis, 4 - r)[0], place * 2 + core],
            spec_piece(axis, r),
            s_q1.at[axis],
            r_q1.at[axis],
            gx,
            d,
        )

    def q1_own(axis, r):
        place = at.x if axis == 0 else at.y
        return pltpu.make_async_copy(
            out1.at[axis, at.across(axis, 4 - r)[0], place * 2 + at.c],
            spec_piece(axis, r),
            own.at[axis, r],
        )

    def inverse_channel(r):
        for axis in range(2):
            if r:
                q2(axis, r).wait_recv()
            rows_of(axis, at.across(axis, 4 - r)[0])
            for m in FAR_FIRST:
                send(q1(axis, r, m), alone=False)
            q1_own(axis, r).start()

    inverse_channel(0)
    inverse_channel(1)
    inverse_channel(3)
    pass_on(0)
    inverse_channel(2)
    loads[13].wait()
    pass_on(1)

    def inverse_columns(half, offsets, last=False):
        blocks = [at.gy(offset) for offset in offsets]
        table = tuple(jnp.concatenate([yia[k, e] for e in blocks], axis=0) for k in range(2))

        def one(k, carry):
            lanes = pl.ds(256 * k if last else pl.multiple_of(256 * k, 256), 256)
            modes = jnp.concatenate([gather[e, half, :, lanes] for e in blocks], axis=0)
            both = dot3(split(modes), table, TN)
            first_channel = 2 * (8 * half + 2 * k)
            for n, channel in enumerate((0, 32, 1, 33, 2, 34, 3, 35)):
                u[first_channel + channel] = u[first_channel + channel] + both[32 * n : 32 * n + 32]
            return carry

        if not last:
            lax.fori_loop(0, 4, one, 0)
            return
        for k in range(4):
            one(k, 0)
            for low in range(2):
                put(16 * half + 4 * k + 32 * low, 4, 2 + 8 * half + 2 * k + low)

    def put(first_channel, count, k):
        copy = pltpu.make_async_copy(
            u.at[pl.ds(first_channel, count)], result.at[pl.ds(first_channel, count)], done.at[k]
        )
        copy.start()
        pending.append(copy.wait)

    for half in range(2):
        inverse_columns(half, (0, -1, 1, -2, 2))
    pass_on(2)
    for half in range(2):
        inverse_columns(half, (-3, 3))
    for axis in range(2):
        bytes_of(spec.at[axis, :, pl.ds(0, 7)], r_q1.at[axis]).wait()
        for r in range(4):
            q1_own(axis, r).wait()

        def add(k, carry):
            if axis == 0:
                here = pl.ds(64 + 8 * k, 8)
                u[here] = u[here] + spec[0, k]
            else:
                for place in range(4):
                    here = pl.ds(96 + 8 * k + 2 * place, 2)
                    u[here] = u[here] + spec[1, place, pl.ds(2 * k, 2)]
            return carry

        lax.fori_loop(0, 4, add, 0)
        put(64 + 32 * axis, 32, axis)
    pass_on(3)
    for half in range(2):
        inverse_columns(half, (4,), last=True)
    drain()
    for axis in range(2):
        bytes_of(out1.at[axis, :, pl.ds(0, 7)], s_q1.at[axis]).wait()
    bytes_of(ring.at[pl.ds(0, 3)], s_g.at[0]).wait()
    bytes_of(ring.at[3, pl.ds(0, 2)], s_g.at[0]).wait()


def spectral_call(grid_field, coefficient, spectral_weight, local_weight, consts):
    dma = pltpu.SemaphoreType.DMA
    vmem = pltpu.VMEM
    scratch = [
        vmem((2, 2, 256, 256), bf16),
        vmem((2, 2, 512, 128), bf16),
        vmem((2, 256, 256), bf16),
        vmem((2, 256, 256), bf16),
        vmem((2, 8, 32, 256), bf16),
        vmem((2, 1024, 256), bf16),
        vmem((2, 128, 2048), bf16),
        vmem((4096, 128), f32),
        vmem((4096, 128), bf16),
        vmem((4096, 128), bf16),
        vmem((2, 512, 512), bf16),
        vmem((64, 64), f32),
        vmem((32, 256), f32),
        vmem((128, 32, 256), f32),
        vmem((128, 32, 256), f32),
        vmem((2, 128, 256), f32),
        vmem((2, 128, 256), f32),
        vmem((2, 16, 1, 256), f32),
        vmem((2, 16, 1, 256), f32),
        vmem((8, 2, 32, 1024), f32),
        vmem((4, 4, 32, 1024), f32),
        vmem((2, 4, 8, 32, 256), f32),
        vmem((2, 4, 8, 2, 16, 128), f32),
        vmem((2, 4, 8, 2, 16, 128), f32),
        vmem((8, 2, 2, 16, 128), f32),
        vmem((4, 4, 2, 16, 128), f32),
        vmem((32, 16, 128), f32),
        vmem((32, 16, 128), f32),
        vmem((2, 32, 4, 128), f32),
        vmem((2, 32, 4, 128), f32),
        vmem((2, 32, 4, 128), f32),
        vmem((2, 32, 4, 128), f32),
        vmem((32, 16, 128), f32),
        vmem((32, 16, 128), f32),
        vmem((2, 2, 16, 128), f32),
        vmem((8, 2, 2, 16, 128), f32),
        vmem((2, 4, 8, 2, 16, 128), f32),
        vmem((2, 4, 8, 32, 256), f32),
        vmem((8, 2, 32, 1024), f32),
        vmem((2, 4, 8, 32, 256), f32),
        dma((14,)),
        dma((2,)),
        dma((2, 4)),
        dma((2, 4)),
        dma((2, 4)),
        dma((4, 4)),
        dma((4, 4)),
        dma((1,)),
        dma((4, 4, 2)),
        *[dma((1,)) for _ in range(2)],
        *[dma((2, 1)) for _ in range(4)],
        *[dma((1,)) for _ in range(2)],
        dma((1,)),
        dma((4, 4, 2)),
        dma((8,)),
        dma((8,)),
        dma((2, 4)),
        dma((2, 4)),
        dma((2,)),
        dma((2,)),
        *[dma((2,)) for _ in range(4)],
        dma((2, 4)),
        dma((18,)),
    ]
    hbm = pl.BlockSpec(memory_space=pl.ANY)
    return pl.pallas_call(
        spectral_kernel,
        out_shape=jax.ShapeDtypeStruct((128, 32, 256), f32),
        in_specs=[hbm] * 12,
        out_specs=hbm,
        scratch_shapes=scratch,
        compiler_params=pltpu.CompilerParams(
            collective_id=0, has_side_effects=True, vmem_limit_bytes=56 << 20
        ),
        name="spectral",
    )(
        grid_field.reshape(2, 2, 4, 4, 2, 32, 256),
        grid_field.reshape(128, 32, 256),
        spectral_weight.reshape(4096, 128),
        local_weight,
        coefficient,
        *consts,
    )


def kernel_only(consts, grid_field, coefficient, spectral_weight, local_weight):
    consts = [jnp.asarray(c) for c in consts]
    return spectral_call(grid_field, coefficient, spectral_weight, local_weight, consts)


def gelu_kernel(sums, result):
    result[...] = jax.nn.gelu(sums[...])


def shards(consts, *arguments):
    block = pl.BlockSpec((32, 32, 256), lambda k: (k, 0, 0))
    result = pl.pallas_call(
        gelu_kernel,
        grid=(4,),
        in_specs=[block],
        out_specs=block,
        out_shape=jax.ShapeDtypeStruct((128, 32, 256), f32),
        compiler_params=pltpu.CompilerParams(vmem_limit_bytes=56 << 20),
        name="gelu",
    )(kernel_only(consts, *arguments))
    return result.reshape(2, 64, 32, 256)


def solution(mesh):
    consts = tables()
    placed = (P(None, None, "gx", "gy"), P("gx", "gy"), P("gx", "gy", None, None), P())
    return jax.shard_map(
        functools.partial(shards, consts),
        mesh=mesh,
        in_specs=placed,
        out_specs=P(None, None, "gx", "gy"),
        check_vma=False,
    )
```
